128 devices in a mesh: row: 8 (over y_lo, z), col: 16 (over x, y_hi, core).
Axes of the slice: x: 4, y: 4 (y_hi: 2, y_lo: 2; y = y_hi * 2 + y_lo), z: 4, core: 2. Of those that a mesh axis runs over, the one named last changes fastest.
Arguments:
- pair: float32 [512, 512, 128], P('row', 'col'), may hold values from -6 to 6
- norm_gain: float32 [2, 2, 128], replicated, may hold values from 0.1 to 1.9
- proj_weight: bfloat16 [2, 128, 640], replicated, may hold values from -0.5 to 0.5
- out_weight: bfloat16 [2, 128, 128], replicated, may hold values from -0.5 to 0.5
Outputs:
- updated_pair: float32 [512, 512, 128], P('row', 'col')
The draws below stay inside these ranges and needn't reach their ends.
All inputs are finite; a program needn't handle non-finite values.
Results may differ from the reference program's by a relative error of at most 0.0055.
Values may be sent and summed in bfloat16 or wider, within the bound.
A program may use at most 128 MiB of HBM per device.

```python
import jax
import jax.numpy as jnp
from jax import lax

C = 128
CH = 128
N = 512


def block_levels(own_key, dims, split, least, largest):
    factor_of, own = 1.0, jax.random.fold_in(own_key, 6)
    for axis_at, parts in split:
        steps = jnp.exp(jax.random.uniform(jax.random.fold_in(own, axis_at), (parts,), jnp.float32, least / len(split), largest / len(split)))
        factor_of = factor_of * jnp.repeat(steps, dims[axis_at] // parts).reshape([-1 if axis == axis_at else 1 for axis in range(len(dims))])
    return factor_of


def gaussian(own_key, extent, scale, reach, shards=(), dtype=jnp.bfloat16):
    factor_of = block_levels(own_key, extent, shards, -0.22, 0.18) if shards else 1.0
    drawn = jax.random.normal(own_key, extent, jnp.float32) * scale * factor_of
    return jnp.minimum(jnp.maximum(drawn, -reach), reach).astype(dtype)


def setup_inputs(seed: int = 0) -> dict:
    arg_keys = jax.random.split(jax.random.key(seed), 5)
    return {
        "pair": gaussian(arg_keys[0], (N, N, C), 1.0, 6.0, ((0, 8), (1, 16)), jnp.float32),
        "norm_gain": jnp.clip(1.0 + 0.18 * jax.random.normal(arg_keys[1], (2, 2, C), jnp.float32), 0.1, 1.9),
        "proj_weight": gaussian(arg_keys[2], (2, C, 5 * CH), C ** -0.5, 0.5),
        "out_weight": gaussian(arg_keys[3], (2, CH, C), CH ** -0.5, 0.5),
    }


def layer_norm(values, scale_gain):
    center = lax.optimization_barrier(jnp.mean(values, axis=-1, keepdims=True))
    shifted = values - center
    spread = lax.optimization_barrier(jnp.mean(shifted * shifted, axis=-1, keepdims=True))
    return shifted * lax.rsqrt(spread + 1e-05) * scale_gain

def project_pair(pair_state, scale_gain, proj_matrix):
    rows, cols, chan = pair_state.shape
    hidden = proj_matrix.shape[1] // 5
    normed = layer_norm(pair_state, scale_gain).astype(jnp.bfloat16).reshape(rows * cols, chan)
    proj = jnp.dot(normed, proj_matrix, preferred_element_type=jnp.float32).reshape(rows, cols, 5 * hidden)
    left_edge = (jax.nn.sigmoid(proj[..., 0:hidden]) * proj[..., hidden:2 * hidden]).astype(jnp.bfloat16)
    right_edge = (jax.nn.sigmoid(proj[..., 2 * hidden:3 * hidden]) * proj[..., 3 * hidden:4 * hidden]).astype(jnp.bfloat16)
    out_gate = jax.nn.sigmoid(proj[..., 4 * hidden:5 * hidden])
    return (left_edge, right_edge, out_gate)

def finish_update(pair_state, product, scale_gain, out_matrix, out_gate):
    rows, cols, hidden = product.shape
    outnorm = layer_norm(product, scale_gain).astype(jnp.bfloat16).reshape(rows * cols, hidden)
    mapped = jnp.dot(outnorm, out_matrix, preferred_element_type=jnp.float32).reshape(rows, cols, -1)
    return pair_state + out_gate * mapped

def reference(pair, norm_gain, proj_weight, out_weight):
    state = pair
    left_edge, right_edge, out_gate = project_pair(state, norm_gain[0, 0], proj_weight[0])
    product = jnp.einsum('ikc,jkc->ijc', left_edge.astype(jnp.float32), right_edge.astype(jnp.float32), precision=lax.Precision.HIGHEST)
    state = finish_update(state, product, norm_gain[0, 1], out_weight[0], out_gate)
    left_edge, right_edge, out_gate = project_pair(state, norm_gain[1, 0], proj_weight[1])
    product = jnp.einsum('kic,kjc->ijc', left_edge.astype(jnp.float32), right_edge.astype(jnp.float32), precision=lax.Precision.HIGHEST)
    state = finish_update(state, product, norm_gain[1, 1], out_weight[1], out_gate)
    return state
```

```python
import functools

import jax
import jax.numpy as jnp
from jax import lax
from jax.experimental import pallas as pl
from jax.experimental.pallas import tpu as pltpu
from jax.sharding import PartitionSpec as P

MESH = pl.DeviceIdType.MESH
ROWS, COLS = 8, 16
DEV = ROWS * COLS
A, B = 64, 32
CH = 128
POS = A * B
TILES = 16
N = 512


def sigmoid(x):
    return 0.5 * jnp.tanh(0.5 * x) + 0.5


def layer_norm(x):
    center = jnp.mean(x, axis=-1, keepdims=True)
    shifted = x - center
    spread = jnp.mean(shifted * shifted, axis=-1, keepdims=True)
    return shifted * lax.rsqrt(spread + 1e-05)


def swap_halves(v0, v1):
    h = CH // 2
    return (
        jnp.concatenate([v0[:, :h], v1[:, :h]], axis=1),
        jnp.concatenate([v0[:, h:], v1[:, h:]], axis=1),
    )


def kernel(pair, gain, weight, weight_out, out, state, normed, gate, wt, wide, send, recv, xl, xr,
           tri_send, tri_recv, stats, send_sem, recv_sem):
    r, c = lax.axis_index("row"), lax.axis_index("col")
    me = r * COLS + c

    def partner(t):
        d = lax.rem(me + t, DEV)
        return d, (lax.div(d, COLS), lax.rem(d, COLS))

    barrier = pltpu.get_barrier_semaphore()

    def greet(t, _):
        pl.semaphore_signal(barrier, inc=1, device_id=partner(t)[1], device_id_type=MESH)
        return 0

    lax.fori_loop(1, DEV, greet, 0)

    def exchange(src, dst, step):
        def send_one(t, _):
            d, dev = partner(t)
            pltpu.make_async_remote_copy(
                src_ref=src.at[d], dst_ref=dst.at[me], send_sem=send_sem.at[step],
                recv_sem=recv_sem.at[step], device_id=dev, device_id_type=MESH,
            ).start()
            return 0

        lax.fori_loop(1, DEV, send_one, 0)
        pltpu.make_async_copy(src.at[me], dst.at[me], recv_sem.at[step]).start()

    def arrived(dst, step):
        pltpu.make_async_copy(dst, dst, recv_sem.at[step]).wait()

    def left(src, step):
        rest = src.at[pl.ds(0, DEV - 1)]
        pltpu.make_async_copy(rest, rest, send_sem.at[step]).wait()

    for s in range(TILES):
        for p in range(2):
            state[pl.ds(s * CH + p * A, A), :] = pair[pl.ds(p * TILES + s, A, stride=B), :]

    for u in range(2):
        wt[...] = jnp.transpose(weight[u, :, 0 : 4 * CH])

        def project(n, _):
            at = pl.ds(pl.multiple_of(n * 256, 256), 256)
            rows = (layer_norm(state[at, :]) * gain[2 * u : 2 * u + 1, :]).astype(jnp.bfloat16)
            normed[at, :] = rows
            proj = lax.dot_general(
                wt[...], rows, (((1,), (1,)), ((), ())), preferred_element_type=jnp.float32
            )
            le = sigmoid(proj[0:CH]) * proj[CH : 2 * CH]
            ri = sigmoid(proj[2 * CH : 3 * CH]) * proj[3 * CH : 4 * CH]
            for h in range(2):
                s = n * 2 + h
                wide[pl.ds(s, CH, stride=32), :] = le[:, h * CH : (h + 1) * CH]
                wide[pl.ds(TILES + s, CH, stride=32), :] = ri[:, h * CH : (h + 1) * CH]
            return 0

        lax.fori_loop(0, 8, project, 0)
        if u == 0:
            pl.semaphore_wait(barrier, DEV - 1)
        else:
            left(send, 0)

        def pack(n, _):
            send[pl.ds(n * 16, 16)] = (
                wide[pl.ds(pl.multiple_of(n * 512, 512), 512), :].astype(jnp.bfloat16).reshape(16, 32, CH)
            )
            return 0

        lax.fori_loop(0, 8, pack, 0)
        exchange(send, recv.at[u], 2 * u)

        def open_gate(n, _):
            at = pl.ds(pl.multiple_of(n * 256, 256), 256)
            gate[at, :] = sigmoid(
                jnp.dot(normed[at, :], weight[u, :, 4 * CH : 5 * CH], preferred_element_type=jnp.float32)
            )
            return 0

        lax.fori_loop(0, 8, open_gate, 0)
        gain_out = jnp.transpose(jnp.broadcast_to(gain[2 * u + 1 : 2 * u + 2, :], (CH, CH)))
        arrived(recv.at[u], 2 * u)

        def join(cc, _):
            for rp in range(4):
                t0 = recv[u, 2 * rp * COLS + cc]
                t1 = recv[u, (2 * rp + 1) * COLS + cc]
                for x, lo in ((xl, 0), (xr, TILES)):
                    p0, p1 = swap_halves(t0[lo : lo + TILES], t1[lo : lo + TILES])
                    x[pl.ds(pl.multiple_of(cc * B, B), TILES), rp * CH : (rp + 1) * CH] = p0
                    x[pl.ds(pl.multiple_of(cc * B + TILES, TILES), TILES), rp * CH : (rp + 1) * CH] = p1
            return 0

        lax.fori_loop(0, COLS, join, 0)

        over = 0 if u == 0 else 1
        if u == 1:
            left(tri_send, 1)
        for h in range(4):
            if u == 0:
                lhs = xr[:, h * CH : (h + 1) * CH]
            else:
                lhs = xr[h * CH : (h + 1) * CH, :]
            tri = lax.dot_general(
                lhs, xl[...], (((over,), (over,)), ((), ())), preferred_element_type=jnp.float32
            ).astype(jnp.bfloat16)
            for i in range(4):
                cc = h * 4 + i
                for rp in range(4):
                    q0 = tri[i * B : i * B + TILES, rp * CH : (rp + 1) * CH]
                    q1 = tri[i * B + TILES : (i + 1) * B, rp * CH : (rp + 1) * CH]
                    p0, p1 = swap_halves(q0, q1)
                    tri_send[2 * rp * COLS + cc] = p0
                    tri_send[(2 * rp + 1) * COLS + cc] = p1
        exchange(tri_send, tri_recv.at[u], 2 * u + 1)
        arrived(tri_recv.at[u], 2 * u + 1)

        def add(n, acc):
            return acc + tri_recv[u, pl.ds(n * 8, 8)].astype(jnp.float32).sum(axis=0)

        center = lax.fori_loop(0, 16, add, jnp.zeros((TILES, CH), jnp.float32)) * (1.0 / CH)

        def add_square(n, acc):
            x = tri_recv[u, pl.ds(n * 8, 8)].astype(jnp.float32) - center
            return acc + (x * x).sum(axis=0)

        spread = lax.fori_loop(0, 16, add_square, jnp.zeros((TILES, CH), jnp.float32)) * (1.0 / CH)
        inv = lax.rsqrt(spread + 1e-05)

        def scale(n, _):
            x = (tri_recv[u, pl.ds(n * 8, 8)].astype(jnp.float32) - center) * inv
            wide[pl.ds(pl.multiple_of(n * 128, 128), 128), :] = x.reshape(8 * TILES, CH)
            return 0

        lax.fori_loop(0, 16, scale, 0)
        stats[...] = gain_out
        for s in range(TILES):
            outnorm = (wide[pl.ds(s, CH, stride=TILES), :] * stats[...]).astype(jnp.bfloat16)
            mapped = lax.dot_general(
                outnorm, weight_out[u], (((0,), (0,)), ((), ())), preferred_element_type=jnp.float32
            )
            at = pl.ds(s * CH, CH)
            new = state[at, :] + gate[at, :] * mapped
            if u == 0:
                state[at, :] = new
            else:
                for p in range(2):
                    out[pl.ds(p * TILES + s, A, stride=B), :] = new[p * A : (p + 1) * A]
    left(send, 2)
    left(tri_send, 3)


def shards(pair, gain, weight, weight_out):
    vmem = pl.BlockSpec(memory_space=pltpu.VMEM)
    f32, bf16 = jnp.float32, jnp.bfloat16
    result = pl.pallas_call(
        kernel,
        out_shape=jax.ShapeDtypeStruct((POS, CH), f32),
        in_specs=[vmem] * 4,
        out_specs=vmem,
        scratch_shapes=[
            pltpu.VMEM((POS, CH), f32),
            pltpu.VMEM((POS, CH), bf16),
            pltpu.VMEM((POS, CH), f32),
            pltpu.VMEM((4 * CH, CH), bf16),
            pltpu.VMEM((2 * POS, CH), f32),
            pltpu.VMEM((DEV, 2 * TILES, CH), bf16),
            pltpu.VMEM((2, DEV, 2 * TILES, CH), bf16),
            pltpu.VMEM((N, N), bf16),
            pltpu.VMEM((N, N), bf16),
            pltpu.VMEM((DEV, TILES, CH), bf16),
            pltpu.VMEM((2, DEV, TILES, CH), bf16),
            pltpu.VMEM((CH, CH), f32),
            pltpu.SemaphoreType.DMA((4,)),
            pltpu.SemaphoreType.DMA((4,)),
        ],
        compiler_params=pltpu.CompilerParams(
            collective_id=0, has_side_effects=True, vmem_limit_bytes=40 << 20
        ),
    )(pair.reshape(POS, CH), gain.reshape(4, CH), weight, weight_out)
    return result.reshape(A, B, CH)


def solution(mesh):
    placed = (P("row", "col", None), P(), P(), P())
    return jax.shard_map(
        shards, mesh=mesh, in_specs=placed, out_specs=P("row", "col", None), check_vma=False
    )
```

```python
import jax
import jax.numpy as jnp
from jax import lax
from jax.experimental import pallas as pl
from jax.experimental.pallas import tpu as pltpu
from jax.sharding import PartitionSpec as P

MESH = pl.DeviceIdType.MESH
ROWS, COLS = 8, 16
DEV = ROWS * COLS
CHIPS = DEV // 2
A, B = 64, 32
CH = 128
POS = A * B
TILES = 16
N = 512
GROUPS = 2
PER = CH // GROUPS
WIDE = 512
STEPS = POS // WIDE
SUB = WIDE // CH


def sigmoid(x):
    return 0.5 * jnp.tanh(0.5 * x) + 0.5


def layer_norm(x, gain):
    center = jnp.mean(x, axis=0, keepdims=True)
    shifted = x - center
    spread = jnp.mean(shifted * shifted, axis=0, keepdims=True)
    return shifted * lax.rsqrt(spread + 1e-05) * gain


def swap_halves(v0, v1):
    h = CH // 2
    return (
        jnp.concatenate([v0[:, :h], v1[:, :h]], axis=1),
        jnp.concatenate([v0[:, h:], v1[:, h:]], axis=1),
    )


def dot(a, b):
    return jnp.dot(a, b, preferred_element_type=jnp.float32)


def kernel(pair_in, gain_in, weight_in, weight_out_in, out, pair, gain, weight, weight_out, state,
           normed, gate, wt, wot, gcol, wide, send, recv, xl, xr, tri_send, tri_recv, in_sem,
           send_sem, recv_sem, met_sem):
    r, c = lax.axis_index("row"), lax.axis_index("col")
    me = r * COLS + c
    chip, core = lax.div(me, 2), lax.rem(me, 2)
    mine = core * PER + chip

    loads = [
        pltpu.make_async_copy(x, y, in_sem.at[i])
        for i, (x, y) in enumerate(
            ((weight_in, weight), (gain_in, gain), (pair_in, pair), (weight_out_in, weight_out))
        )
    ]
    for load in loads:
        load.start()

    barrier = pltpu.get_barrier_semaphore()
    for t in range(1, ROWS):
        pl.semaphore_signal(barrier, inc=1, device_id=(lax.rem(r + t, ROWS), c), device_id_type=MESH)
    for t in range(1, COLS):
        pl.semaphore_signal(barrier, inc=1, device_id=(r, lax.rem(c + t, COLS)), device_id_type=MESH)

    def ready():
        pl.semaphore_wait(barrier, ROWS + COLS - 2)
        for t in range(1, ROWS):
            pl.semaphore_signal(met_sem, inc=1, device_id=(lax.rem(r + t, ROWS), c), device_id_type=MESH)
        pl.semaphore_wait(met_sem, ROWS - 1)

    x, y, z = lax.div(c, 4), lax.rem(lax.div(c, 2), 2) * 2 + lax.div(r, 4), lax.rem(r, 4)

    def far_first(q):
        return 2 + q - lax.div(q, 2) * (2 * q - 1)

    def partner(t, g):
        dx = lax.rem(x + far_first(lax.rem(t, 4)), 4)
        dy = lax.rem(y + far_first(lax.rem(lax.div(t, 4), 4)), 4)
        dz = lax.rem(z + far_first(lax.div(t, 16)), 4)
        row = lax.rem(dy, 2) * 4 + dz
        col = dx * 4 + lax.div(dy, 2) * 2 + g
        d = row * COLS + col
        return d, g * PER + lax.div(d, 2), (row, col)

    def remote(src, dst, step, dev):
        pltpu.make_async_remote_copy(
            src_ref=src, dst_ref=dst, send_sem=send_sem.at[step],
            recv_sem=recv_sem.at[step], device_id=dev, device_id_type=MESH,
        ).start()

    def local(src, dst, step):
        pltpu.make_async_copy(src, dst, recv_sem.at[step]).start()

    def spread_channels(g, u):
        def one(t, _):
            d, ch, dev = partner(t, g)
            remote(send.at[ch], recv.at[u, me], 2 * u, dev)
            return 0

        lax.fori_loop(0, CHIPS - 1, one, 0)
        d, ch, dev = partner(CHIPS - 1, g)

        @pl.when(core == g)
        def _():
            local(send.at[ch], recv.at[u, me], 2 * u)

        @pl.when(core != g)
        def _():
            remote(send.at[ch], recv.at[u, me], 2 * u, dev)

    def spread_tri(g, u):
        def one(t, _):
            d, ch, dev = partner(t, g)
            remote(tri_send.at[d], tri_recv.at[u, mine], 2 * u + 1, dev)
            return 0

        lax.fori_loop(0, CHIPS - 1, one, 0)
        d, ch, dev = partner(CHIPS - 1, g)

        @pl.when(core == g)
        def _():
            local(tri_send.at[d], tri_recv.at[u, mine], 2 * u + 1)

        @pl.when(core != g)
        def _():
            remote(tri_send.at[d], tri_recv.at[u, mine], 2 * u + 1, dev)

    def arrived(dst, step):
        pltpu.make_async_copy(dst, dst, recv_sem.at[step]).wait()

    def left(src, step):
        rest = src.at[pl.ds(0, DEV - 1)]
        pltpu.make_async_copy(rest, rest, send_sem.at[step]).wait()

    def turn(u):
        whole = jnp.transpose(weight[u])
        for g in range(GROUPS):
            for k in range(4):
                wt[u, (4 * g + k) * PER : (4 * g + k + 1) * PER] = whole[k * CH + g * PER : k * CH + (g + 1) * PER]
        wt[u, 4 * CH :] = whole[4 * CH :]
        wot[u] = jnp.transpose(weight_out[u])
        for k in range(2):
            gcol[2 * u + k] = jnp.transpose(jnp.broadcast_to(gain[2 * u + k : 2 * u + k + 1, :], (CH, CH)))

    loads[0].wait()
    loads[1].wait()
    loads[3].wait()
    turn(0)
    loads[2].wait()
    for s in range(TILES):
        rows = jnp.concatenate([pair[pl.ds(p * TILES + s, A, stride=B), :] for p in range(2)], axis=0)
        turned = jnp.transpose(rows)
        state[:, s * CH : (s + 1) * CH] = turned
        normed[:, s * CH : (s + 1) * CH] = layer_norm(turned, gcol[0]).astype(jnp.bfloat16)

    for u in range(2):
        for g in range(GROUPS):
            w = wt[u, 4 * PER * g : 4 * PER * (g + 1)]

            def project(n, _):
                at = pl.ds(pl.multiple_of(n * WIDE, WIDE), WIDE)
                proj = dot(w, normed[:, at])
                le = sigmoid(proj[0:PER]) * proj[PER : 2 * PER]
                ri = sigmoid(proj[2 * PER : 3 * PER]) * proj[3 * PER : 4 * PER]
                for h in range(SUB):
                    s = n * SUB + h
                    wide[pl.ds(s, PER, stride=32), :] = le[:, h * CH : (h + 1) * CH]
                    wide[pl.ds(TILES + s, PER, stride=32), :] = ri[:, h * CH : (h + 1) * CH]
                return 0

            lax.fori_loop(0, STEPS, project, 0)
            if g == 0:
                if u == 0:
                    ready()
                else:
                    left(send, 0)

            def pack(n, _):
                send[pl.ds(g * PER + n * 16, 16)] = (
                    wide[pl.ds(pl.multiple_of(n * 512, 512), 512), :].astype(jnp.bfloat16).reshape(16, 32, CH)
                )
                return 0

            lax.fori_loop(0, PER // 16, pack, 0)
            spread_channels(g, u)

        def open_gate(n, _):
            at = pl.ds(pl.multiple_of(n * WIDE, WIDE), WIDE)
            gate[:, at] = sigmoid(dot(wt[u, 4 * CH :], normed[:, at]))
            return 0

        lax.fori_loop(0, STEPS, open_gate, 0)
        if u == 0:
            turn(1)
        arrived(recv.at[u], 2 * u)

        def join(cc, _):
            for rp in range(4):
                t0 = recv[u, 2 * rp * COLS + cc]
                t1 = recv[u, (2 * rp + 1) * COLS + cc]
                for x, lo in ((xl, 0), (xr, TILES)):
                    p0, p1 = swap_halves(t0[lo : lo + TILES], t1[lo : lo + TILES])
                    x[pl.ds(pl.multiple_of(cc * B, B), TILES), rp * CH : (rp + 1) * CH] = p0
                    x[pl.ds(pl.multiple_of(cc * B + TILES, TILES), TILES), rp * CH : (rp + 1) * CH] = p1
            return 0

        lax.fori_loop(0, COLS, join, 0)

        over = 0 if u == 0 else 1
        if u == 1:
            left(tri_send, 1)
        for h in range(4):
            if u == 0:
                lhs = xr[:, h * CH : (h + 1) * CH]
            else:
                lhs = xr[h * CH : (h + 1) * CH, :]
            tri = lax.dot_general(
                lhs, xl[...], (((over,), (over,)), ((), ())), preferred_element_type=jnp.float32
            ).astype(jnp.bfloat16)
            for i in range(4):
                cc = h * 4 + i
                for rp in range(4):
                    q0 = tri[i * B : i * B + TILES, rp * CH : (rp + 1) * CH]
                    q1 = tri[i * B + TILES : (i + 1) * B, rp * CH : (rp + 1) * CH]
                    p0, p1 = swap_halves(q0, q1)
                    tri_send[2 * rp * COLS + cc] = p0
                    tri_send[(2 * rp + 1) * COLS + cc] = p1
        for g in range(GROUPS):
            spread_tri(g, u)
        arrived(tri_recv.at[u], 2 * u + 1)

        def unpack(n, _):
            x = tri_recv[u, pl.ds(n * 16, 16)].astype(jnp.float32)
            wide[pl.ds(pl.multiple_of(n * 256, 256), 256), :] = x.reshape(16 * TILES, CH)
            return 0

        lax.fori_loop(0, CH // 16, unpack, 0)

        def finish(n, _):
            at = pl.ds(pl.multiple_of(n * WIDE, WIDE), WIDE)
            outnorm = [
                layer_norm(wide[pl.ds(n * SUB + h, CH, stride=TILES), :], gcol[2 * u + 1]).astype(jnp.bfloat16)
                for h in range(SUB)
            ]
            new = state[:, at] + gate[:, at] * dot(wot[u], jnp.concatenate(outnorm, axis=1))
            if u == 0:
                state[:, at] = new
            for h in range(SUB):
                part = new[:, h * CH : (h + 1) * CH]
                if u == 0:
                    normed[:, pl.ds(pl.multiple_of(n * WIDE + h * CH, CH), CH)] = layer_norm(part, gcol[2]).astype(jnp.bfloat16)
                else:
                    rows = jnp.transpose(part)
                    for p in range(2):
                        out[pl.ds(p * TILES + n * SUB + h, A, stride=B), :] = rows[p * A : (p + 1) * A]
            return 0

        lax.fori_loop(0, STEPS, finish, 0)
    left(send, 2)
    left(tri_send, 3)


def shards(pair, gain, weight, weight_out):
    hbm = pl.BlockSpec(memory_space=pltpu.HBM)
    f32, bf16 = jnp.float32, jnp.bfloat16
    result = pl.pallas_call(
        kernel,
        out_shape=jax.ShapeDtypeStruct((POS, CH), f32),
        in_specs=[hbm] * 4,
        out_specs=pl.BlockSpec(memory_space=pltpu.VMEM),
        scratch_shapes=[
            pltpu.VMEM((POS, CH), f32),
            pltpu.VMEM((4, CH), f32),
            pltpu.VMEM((2, CH, 5 * CH), bf16),
            pltpu.VMEM((2, CH, CH), bf16),
            pltpu.VMEM((CH, POS), f32),
            pltpu.VMEM((CH, POS), bf16),
            pltpu.VMEM((CH, POS), f32),
            pltpu.VMEM((2, 5 * CH, CH), bf16),
            pltpu.VMEM((2, CH, CH), bf16),
            pltpu.VMEM((4, CH, CH), f32),
            pltpu.VMEM((POS, CH), f32),
            pltpu.VMEM((DEV, 2 * TILES, CH), bf16),
            pltpu.VMEM((2, DEV, 2 * TILES, CH), bf16),
            pltpu.VMEM((N, N), bf16),
            pltpu.VMEM((N, N), bf16),
            pltpu.VMEM((DEV, TILES, CH), bf16),
            pltpu.VMEM((2, DEV, TILES, CH), bf16),
            pltpu.SemaphoreType.DMA((4,)),
            pltpu.SemaphoreType.DMA((4,)),
            pltpu.SemaphoreType.DMA((4,)),
            pltpu.SemaphoreType.REGULAR,
        ],
        compiler_params=pltpu.CompilerParams(
            collective_id=0, has_side_effects=True, vmem_limit_bytes=58 << 20
        ),
    )(pair.reshape(POS, CH), gain.reshape(4, CH), weight, weight_out)
    return result.reshape(A, B, CH)


def solution(mesh):
    placed = (P("row", "col", None), P(), P(), P())
    return jax.shard_map(
        shards, mesh=mesh, in_specs=placed, out_specs=P("row", "col", None), check_vma=False
    )
```

```python
import jax
import jax.numpy as jnp
from jax import lax
from jax.experimental import pallas as pl
from jax.experimental.pallas import tpu as pltpu
from jax.sharding import PartitionSpec as P

LOGICAL = pl.DeviceIdType.LOGICAL
FAR_FIRST = (2, 3, 1, 0)
ROWS, COLS = 8, 16
DEV = ROWS * COLS
CHIPS = DEV // 2
A, B = 64, 32
CH = 128
POS = A * B
TILES = 16
N = 512
GROUPS = 2
PER = CH // GROUPS
WIDE = 512
STEPS = POS // WIDE
PLANE = DEV // 4
SUB = WIDE // CH


def sigmoid(x):
    return 0.5 * jnp.tanh(0.5 * x) + 0.5


def layer_norm(x, gain):
    center = jnp.mean(x, axis=0, keepdims=True)
    shifted = x - center
    spread = jnp.mean(shifted * shifted, axis=0, keepdims=True)
    return shifted * lax.rsqrt(spread + 1e-05) * gain


def swap_halves(v0, v1):
    h = CH // 2
    return (
        jnp.concatenate([v0[:, :h], v1[:, :h]], axis=1),
        jnp.concatenate([v0[:, h:], v1[:, h:]], axis=1),
    )


def dot(a, b):
    return jnp.dot(a, b, preferred_element_type=jnp.float32)


def kernel(pair_in, gain_in, weight_in, weight_out_in, out, pair, gain, weight, weight_out, state,
           normed, gate, wt, wot, gcol, wide, send, recv, xl, xr, tri_send, tri_recv, in_sem,
           send_sem, recv_sem):
    r, c = lax.axis_index("row"), lax.axis_index("col")
    me = r * COLS + c
    chip, core = lax.div(me, 2), lax.rem(me, 2)
    mine = core * PER + chip

    loads = [
        pltpu.make_async_copy(x, y, in_sem.at[i])
        for i, (x, y) in enumerate(
            ((weight_in, weight), (gain_in, gain), (pair_in, pair), (weight_out_in, weight_out))
        )
    ]
    for load in loads:
        load.start()

    x, y, z = lax.div(c, 4), lax.rem(lax.div(c, 2), 2) * 2 + lax.div(r, 4), lax.rem(r, 4)
    along_x = [lax.rem(x + k, 4) * 2 for k in FAR_FIRST]
    along_y = [lax.rem(lax.rem(y + k, 4), 2) * 32 + lax.div(lax.rem(y + k, 4), 2) for k in FAR_FIRST]
    along_z = [lax.rem(z + k, 4) * 8 for k in FAR_FIRST]

    def tour(visit):
        for i in range(4):
            def plane(j, _):
                far = 2 + j - lax.div(j, 2) * (2 * j - 1)
                at = along_x[i] + lax.rem(z + far, 4) * 8
                for k in range(4):
                    visit(at + along_y[k], i)
                return 0

            lax.fori_loop(0, 4 if i < 3 else 3, plane, 0)
        for k in range(3):
            visit(along_x[3] + along_z[3] + along_y[k], 3)

    barrier = pltpu.get_barrier_semaphore()

    def greet(g):
        def visit(other, i):
            pl.semaphore_signal(barrier, inc=1, device_id=other * 2 + g, device_id_type=LOGICAL)

        tour(visit)

    greet(0)
    greet(1)
    pl.semaphore_signal(barrier, inc=1, device_id=chip * 2 + 1 - core, device_id_type=LOGICAL)

    def ready():
        pl.semaphore_wait(barrier, DEV - 1)

    def spread(src, dst, sends, recvs, g):
        def visit(other, i):
            pltpu.make_async_remote_copy(
                src_ref=src(other), dst_ref=dst(i), send_sem=sends, recv_sem=recvs(i),
                device_id=other * 2 + g, device_id_type=LOGICAL,
            ).start()

        tour(visit)

        @pl.when(core == g)
        def _():
            pltpu.make_async_copy(src(chip), dst(3), recvs(3)).start()

        @pl.when(core != g)
        def _():
            visit(chip, 3)

    slot = r * 4 + lax.rem(c, 4)

    def spread_channels(g, u):
        spread(
            lambda other: send.at[g * PER + other], lambda i: recv.at[u, i * PLANE + slot],
            send_sem.at[2 * u], lambda i: recv_sem.at[u, i], g,
        )

    def spread_tri(g, u):
        spread(
            lambda other: tri_send.at[other * 2 + g], lambda i: tri_recv.at[u, mine],
            send_sem.at[2 * u + 1], lambda i: recv_sem.at[u, 4], g,
        )

    def arrived(dst, sem):
        pltpu.make_async_copy(dst, dst, sem).wait()

    def left(src, step):
        rest = src.at[pl.ds(0, DEV - 1)]
        pltpu.make_async_copy(rest, rest, send_sem.at[step]).wait()

    def turn(u):
        whole = jnp.transpose(weight[u])
        for g in range(GROUPS):
            for k in range(4):
                wt[u, (4 * g + k) * PER : (4 * g + k + 1) * PER] = whole[k * CH + g * PER : k * CH + (g + 1) * PER]
        wt[u, 4 * CH :] = whole[4 * CH :]
        wot[u] = jnp.transpose(weight_out[u])
        for k in range(2):
            gcol[2 * u + k] = jnp.transpose(jnp.broadcast_to(gain[2 * u + k : 2 * u + k + 1, :], (CH, CH)))

    loads[0].wait()
    loads[1].wait()
    loads[3].wait()
    turn(0)
    loads[2].wait()
    for s in range(TILES):
        rows = jnp.concatenate([pair[pl.ds(p * TILES + s, A, stride=B), :] for p in range(2)], axis=0)
        turned = jnp.transpose(rows)
        state[:, s * CH : (s + 1) * CH] = turned
        normed[:, s * CH : (s + 1) * CH] = layer_norm(turned, gcol[0]).astype(jnp.bfloat16)

    for u in range(2):
        for g in range(GROUPS):
            w = wt[u, 4 * PER * g : 4 * PER * (g + 1)]

            def project(n, _):
                at = pl.ds(pl.multiple_of(n * WIDE, WIDE), WIDE)
                proj = dot(w, normed[:, at])
                le = sigmoid(proj[0:PER]) * proj[PER : 2 * PER]
                ri = sigmoid(proj[2 * PER : 3 * PER]) * proj[3 * PER : 4 * PER]
                for h in range(SUB):
                    s = n * SUB + h
                    wide[pl.ds(s, PER, stride=32), :] = le[:, h * CH : (h + 1) * CH]
                    wide[pl.ds(TILES + s, PER, stride=32), :] = ri[:, h * CH : (h + 1) * CH]
                return 0

            lax.fori_loop(0, STEPS, project, 0)
            if g == 0:
                if u == 0:
                    ready()
                else:
                    left(send, 0)

            def pack(n, _):
                send[pl.ds(g * PER + n * 16, 16)] = (
                    wide[pl.ds(pl.multiple_of(n * 512, 512), 512), :].astype(jnp.bfloat16).reshape(16, 32, CH)
                )
                return 0

            lax.fori_loop(0, PER // 16, pack, 0)
            spread_channels(g, u)

        def open_gate(n, _):
            at = pl.ds(pl.multiple_of(n * WIDE, WIDE), WIDE)
            gate[:, at] = sigmoid(dot(wt[u, 4 * CH :], normed[:, at]))
            return 0

        lax.fori_loop(0, STEPS, open_gate, 0)
        if u == 0:
            turn(1)
        for i, k in enumerate(FAR_FIRST):
            arrived(recv.at[u, pl.ds(i * PLANE, PLANE)], recv_sem.at[u, i])
            top = lax.rem(x + 4 - k, 4) * CH

            def join(cc, _):
                at = pl.multiple_of(top + cc * B, B)
                for rp in range(4):
                    t0 = recv[u, i * PLANE + 2 * rp * 4 + cc]
                    t1 = recv[u, i * PLANE + (2 * rp + 1) * 4 + cc]
                    for m, lo in ((xl, 0), (xr, TILES)):
                        p0, p1 = swap_halves(t0[lo : lo + TILES], t1[lo : lo + TILES])
                        m[pl.ds(at, TILES), rp * CH : (rp + 1) * CH] = p0
                        m[pl.ds(pl.multiple_of(at + TILES, TILES), TILES), rp * CH : (rp + 1) * CH] = p1
                return 0

            lax.fori_loop(0, 4, join, 0)

        over = 0 if u == 0 else 1
        if u == 1:
            left(tri_send, 1)
        for h in range(4):
            if u == 0:
                lhs = xr[:, h * CH : (h + 1) * CH]
            else:
                lhs = xr[h * CH : (h + 1) * CH, :]
            tri = lax.dot_general(
                lhs, xl[...], (((over,), (over,)), ((), ())), preferred_element_type=jnp.float32
            ).astype(jnp.bfloat16)
            for i in range(4):
                cc = h * 4 + i
                for rp in range(4):
                    q0 = tri[i * B : i * B + TILES, rp * CH : (rp + 1) * CH]
                    q1 = tri[i * B + TILES : (i + 1) * B, rp * CH : (rp + 1) * CH]
                    p0, p1 = swap_halves(q0, q1)
                    tri_send[2 * rp * COLS + cc] = p0
                    tri_send[(2 * rp + 1) * COLS + cc] = p1
        for g in range(GROUPS):
            spread_tri(g, u)
        arrived(tri_recv.at[u], recv_sem.at[u, 4])

        def unpack(n, _):
            x = tri_recv[u, pl.ds(n * 16, 16)].astype(jnp.float32)
            wide[pl.ds(pl.multiple_of(n * 256, 256), 256), :] = x.reshape(16 * TILES, CH)
            return 0

        lax.fori_loop(0, CH // 16, unpack, 0)

        def finish(n, _):
            at = pl.ds(pl.multiple_of(n * WIDE, WIDE), WIDE)
            outnorm = [
                layer_norm(wide[pl.ds(n * SUB + h, CH, stride=TILES), :], gcol[2 * u + 1]).astype(jnp.bfloat16)
                for h in range(SUB)
            ]
            new = state[:, at] + gate[:, at] * dot(wot[u], jnp.concatenate(outnorm, axis=1))
            if u == 0:
                state[:, at] = new
            for h in range(SUB):
                part = new[:, h * CH : (h + 1) * CH]
                if u == 0:
                    normed[:, pl.ds(pl.multiple_of(n * WIDE + h * CH, CH), CH)] = layer_norm(part, gcol[2]).astype(jnp.bfloat16)
                else:
                    rows = jnp.transpose(part)
                    for p in range(2):
                        out[pl.ds(p * TILES + n * SUB + h, A, stride=B), :] = rows[p * A : (p + 1) * A]
            return 0

        lax.fori_loop(0, STEPS, finish, 0)
    left(send, 2)
    left(tri_send, 3)


def shards(pair, gain, weight, weight_out):
    hbm = pl.BlockSpec(memory_space=pltpu.HBM)
    f32, bf16 = jnp.float32, jnp.bfloat16
    result = pl.pallas_call(
        kernel,
        out_shape=jax.ShapeDtypeStruct((POS, CH), f32),
        in_specs=[hbm] * 4,
        out_specs=pl.BlockSpec(memory_space=pltpu.VMEM),
        scratch_shapes=[
            pltpu.VMEM((POS, CH), f32),
            pltpu.VMEM((4, CH), f32),
            pltpu.VMEM((2, CH, 5 * CH), bf16),
            pltpu.VMEM((2, CH, CH), bf16),
            pltpu.VMEM((CH, POS), f32),
            pltpu.VMEM((CH, POS), bf16),
            pltpu.VMEM((CH, POS), f32),
            pltpu.VMEM((2, 5 * CH, CH), bf16),
            pltpu.VMEM((2, CH, CH), bf16),
            pltpu.VMEM((4, CH, CH), f32),
            pltpu.VMEM((POS, CH), f32),
            pltpu.VMEM((DEV, 2 * TILES, CH), bf16),
            pltpu.VMEM((2, DEV, 2 * TILES, CH), bf16),
            pltpu.VMEM((N, N), bf16),
            pltpu.VMEM((N, N), bf16),
            pltpu.VMEM((DEV, TILES, CH), bf16),
            pltpu.VMEM((2, DEV, TILES, CH), bf16),
            pltpu.SemaphoreType.DMA((4,)),
            pltpu.SemaphoreType.DMA((4,)),
            pltpu.SemaphoreType.DMA((2, 5)),
        ],
        compiler_params=pltpu.CompilerParams(
            collective_id=0, has_side_effects=True, vmem_limit_bytes=40 << 20
        ),
    )(*[pltpu.with_memory_space_constraint(v, pltpu.HBM) for v in (pair.reshape(POS, CH), gain.reshape(4, CH), weight, weight_out)])
    return result.reshape(A, B, CH)


def solution(mesh):
    placed = (P("row", "col", None), P(), P(), P())
    return jax.shard_map(
        shards, mesh=mesh, in_specs=placed, out_specs=P("row", "col", None), check_vma=False
    )
```

```python
import jax
import jax.numpy as jnp
from jax import lax
from jax.experimental import pallas as pl
from jax.experimental.pallas import tpu as pltpu
from jax.sharding import PartitionSpec as P

LOGICAL = pl.DeviceIdType.LOGICAL
FAR_FIRST = (2, 3, 1, 0)
ROWS, COLS = 8, 16
DEV = ROWS * COLS
CHIPS = DEV // 2
A, B = 64, 32
CH = 128
POS = A * B
TILES = 16
N = 512
PER = 16
WIDE = 512
STEPS = POS // WIDE
PLANE = DEV // 4
SUB = WIDE // CH


def sigmoid(x):
    return 0.5 * jnp.tanh(0.5 * x) + 0.5


def layer_norm(x, gain):
    center = jnp.mean(x, axis=0, keepdims=True)
    shifted = x - center
    spread = jnp.mean(shifted * shifted, axis=0, keepdims=True)
    return shifted * lax.rsqrt(spread + 1e-05) * gain


def swap_halves(v0, v1):
    h = CH // 2
    return (
        jnp.concatenate([v0[:, :h], v1[:, :h]], axis=1),
        jnp.concatenate([v0[:, h:], v1[:, h:]], axis=1),
    )


def dot(a, b):
    return jnp.dot(a, b, preferred_element_type=jnp.float32)


def kernel(pair_in, gain_in, weight_in, weight_out_in, out, pair, gain, weight, weight_out, state,
           normed, gate, wt, wot, gcol, wide, send, recv, xl, xr, turned, tri_send, tri_recv, in_sem,
           send_sem, recv_sem):
    r, c = lax.axis_index("row"), lax.axis_index("col")
    me = r * COLS + c
    chip, core = lax.div(me, 2), lax.rem(me, 2)

    loads = [
        pltpu.make_async_copy(x, y, in_sem.at[i])
        for i, (x, y) in enumerate(
            ((weight_in, weight), (gain_in, gain), (pair_in, pair), (weight_out_in, weight_out))
        )
    ]
    for load in loads:
        load.start()

    x, y, z = lax.div(c, 4), lax.rem(lax.div(c, 2), 2) * 2 + lax.div(r, 4), lax.rem(r, 4)
    mine = (core * 4 + x) * PER + r * 2 + lax.div(y, 2)

    def in_y(k):
        at = lax.rem(y + k, 4)
        lo, hi = lax.rem(at, 2), lax.div(at, 2)
        return lo * 32 + hi, lo * 8 + hi

    along_x = [lax.rem(x + k, 4) for k in FAR_FIRST]
    along_y = [in_y(k) for k in FAR_FIRST]

    def tour(i, visit):
        def stop(far, ks):
            at = lax.rem(z + far, 4)
            for k in ks:
                visit(along_x[i] * 2 + at * 8 + along_y[k][0], at * 2 + along_y[k][1])

        def plane(j, _):
            stop(2 + j - lax.div(j, 2) * (2 * j - 1), range(4))
            return 0

        lax.fori_loop(0, 4 if i < 3 else 3, plane, 0)
        if i == 3:
            stop(0, range(3))

    barrier = pltpu.get_barrier_semaphore()

    def greet(g):
        def visit(other, place):
            pl.semaphore_signal(barrier, inc=1, device_id=other * 2 + g, device_id_type=LOGICAL)

        for i in range(4):
            tour(i, visit)

    greet(0)
    greet(1)
    pl.semaphore_signal(barrier, inc=1, device_id=chip * 2 + 1 - core, device_id_type=LOGICAL)

    def ready():
        pl.semaphore_wait(barrier, DEV - 1)

    def spread(src, dst, sends, recvs, g, i):
        def visit(other, place):
            pltpu.make_async_remote_copy(
                src_ref=src(other, place), dst_ref=dst, send_sem=sends, recv_sem=recvs,
                device_id=other * 2 + g, device_id_type=LOGICAL,
            ).start()

        tour(i, visit)
        if i == 3:
            place = r * 2 + lax.div(y, 2)

            @pl.when(core == g)
            def _():
                pltpu.make_async_copy(src(chip, place), dst, recvs).start()

            @pl.when(core != g)
            def _():
                visit(chip, place)

    slot = r * 4 + lax.rem(c, 4)

    def spread_channels(g, i, u):
        spread(
            lambda other, place: send.at[(g * 4 + i) * PER + place], recv.at[u, i * PLANE + slot],
            send_sem.at[2 * u], recv_sem.at[u, i], g, i,
        )

    def spread_tri(g, i, u):
        spread(
            lambda other, place: tri_send.at[other * 2 + g], tri_recv.at[u, mine],
            send_sem.at[2 * u + 1], recv_sem.at[u, 4], g, i,
        )

    def arrived(dst, sem):
        pltpu.make_async_copy(dst, dst, sem).wait()

    def left(src, step):
        rest = src.at[pl.ds(0, DEV - 1)]
        pltpu.make_async_copy(rest, rest, send_sem.at[step]).wait()

    def turn(u):
        whole = jnp.transpose(weight[u])
        for n in range(CH // PER):
            for k in range(4):
                wt[u, (4 * n + k) * PER : (4 * n + k + 1) * PER] = whole[k * CH + n * PER : k * CH + (n + 1) * PER]
        wt[u, 4 * CH :] = whole[4 * CH :]
        wot[u] = jnp.transpose(weight_out[u])
        for k in range(2):
            gcol[2 * u + k] = jnp.transpose(jnp.broadcast_to(gain[2 * u + k : 2 * u + k + 1, :], (CH, CH)))

    loads[0].wait()
    loads[1].wait()
    loads[3].wait()
    turn(0)
    loads[2].wait()
    for s in range(TILES):
        rows = jnp.concatenate([pair[pl.ds(p * TILES + s, A, stride=B), :] for p in range(2)], axis=0)
        values = jnp.transpose(rows)
        state[:, s * CH : (s + 1) * CH] = values
        normed[:, s * CH : (s + 1) * CH] = layer_norm(values, gcol[0]).astype(jnp.bfloat16)

    for u in range(2):
        for n in range(4):
            g, first = n // 2, n % 2 * 2
            w = jnp.concatenate(
                [
                    wt[u, pl.ds(pl.multiple_of((g * 4 + along_x[i]) * 4 * PER, 4 * PER), 4 * PER), :]
                    for i in (first, first + 1)
                ],
                axis=0,
            )
            base = n % 2 * (POS // 2)
            for m in range(STEPS):
                proj = dot(w, normed[:, m * WIDE : (m + 1) * WIDE])
                for e in range(2):
                    part = [proj[(4 * e + k) * PER : (4 * e + k + 1) * PER] for k in range(4)]
                    both = (sigmoid(part[0]) * part[1], sigmoid(part[2]) * part[3])
                    for h in range(SUB):
                        for k in range(2):
                            wide[pl.ds(base + e * 32 * PER + k * TILES + m * SUB + h, PER, stride=32), :] = (
                                both[k][:, h * CH : (h + 1) * CH]
                            )
            if n == 0:
                if u == 0:
                    ready()
                else:
                    left(send, 0)
            for i in (first, first + 1):
                rows = wide[pl.ds(base + (i - first) * 32 * PER, 32 * PER), :]
                send[(g * 4 + i) * PER : (g * 4 + i + 1) * PER] = rows.astype(jnp.bfloat16).reshape(PER, 32, CH)
                spread_channels(g, i, u)

        def open_gate(n, _):
            at = pl.ds(pl.multiple_of(n * WIDE, WIDE), WIDE)
            gate[:, at] = sigmoid(dot(wt[u, 4 * CH :], normed[:, at]))
            return 0

        lax.fori_loop(0, STEPS, open_gate, 0, unroll=True)
        if u == 0:
            turn(1)
        for i, k in enumerate(FAR_FIRST):
            arrived(recv.at[u, pl.ds(i * PLANE, PLANE)], recv_sem.at[u, i])
            top = lax.rem(x + 4 - k, 4) * CH

            def join(cc, _):
                at = pl.multiple_of(top + cc * B, B)
                for rp in range(4):
                    t0 = recv[u, i * PLANE + 2 * rp * 4 + cc]
                    t1 = recv[u, i * PLANE + (2 * rp + 1) * 4 + cc]
                    for m, lo in ((xl, 0), (xr, TILES)):
                        p0, p1 = swap_halves(t0[lo : lo + TILES], t1[lo : lo + TILES])
                        m[pl.ds(at, TILES), rp * CH : (rp + 1) * CH] = p0
                        m[pl.ds(pl.multiple_of(at + TILES, TILES), TILES), rp * CH : (rp + 1) * CH] = p1
                return 0

            lax.fori_loop(0, 4, join, 0, unroll=True)
            block = pl.ds(pl.multiple_of(top, CH), CH)
            turned[:, block] = jnp.transpose((xr if u == 0 else xl)[block, :])

        if u == 1:
            left(tri_send, 1)
        for h in range(4):
            rows = pl.ds(h * CH, CH)
            if u == 0:
                tri = dot(turned[rows, :], xl[...]).astype(jnp.bfloat16)
            else:
                tri = dot(xr[rows, :], turned[...]).astype(jnp.bfloat16)
            for i in range(4):
                cc = h * 4 + i
                for rp in range(4):
                    q0 = tri[i * B : i * B + TILES, rp * CH : (rp + 1) * CH]
                    q1 = tri[i * B + TILES : (i + 1) * B, rp * CH : (rp + 1) * CH]
                    p0, p1 = swap_halves(q0, q1)
                    tri_send[2 * rp * COLS + cc] = p0
                    tri_send[(2 * rp + 1) * COLS + cc] = p1
        for g in (0, 1) if u == 0 else (1, 0):
            for i in range(4):
                spread_tri(g, i, u)
        arrived(tri_recv.at[u], recv_sem.at[u, 4])

        def unpack(n, _):
            x = tri_recv[u, pl.ds(n * 16, 16)].astype(jnp.float32)
            wide[pl.ds(pl.multiple_of(n * 256, 256), 256), :] = x.reshape(16 * TILES, CH)
            return 0

        lax.fori_loop(0, CH // 16, unpack, 0)

        def finish(n, _):
            at = pl.ds(pl.multiple_of(n * WIDE, WIDE), WIDE)
            outnorm = [
                layer_norm(wide[pl.ds(n * SUB + h, CH, stride=TILES), :], gcol[2 * u + 1]).astype(jnp.bfloat16)
                for h in range(SUB)
            ]
            new = state[:, at] + gate[:, at] * dot(wot[u], jnp.concatenate(outnorm, axis=1))
            if u == 0:
                state[:, at] = new
            for h in range(SUB):
                part = new[:, h * CH : (h + 1) * CH]
                if u == 0:
                    normed[:, pl.ds(pl.multiple_of(n * WIDE + h * CH, CH), CH)] = layer_norm(part, gcol[2]).astype(jnp.bfloat16)
                else:
                    rows = jnp.transpose(part)
                    for p in range(2):
                        out[pl.ds(p * TILES + n * SUB + h, A, stride=B), :] = rows[p * A : (p + 1) * A]
            return 0

        lax.fori_loop(0, STEPS, finish, 0, unroll=True)
    left(send, 2)
    left(tri_send, 3)


def shards(pair, gain, weight, weight_out):
    hbm = pl.BlockSpec(memory_space=pltpu.HBM)
    f32, bf16 = jnp.float32, jnp.bfloat16
    result = pl.pallas_call(
        kernel,
        out_shape=jax.ShapeDtypeStruct((POS, CH), f32),
        in_specs=[hbm] * 4,
        out_specs=pl.BlockSpec(memory_space=pltpu.VMEM),
        scratch_shapes=[
            pltpu.VMEM((POS, CH), f32),
            pltpu.VMEM((4, CH), f32),
            pltpu.VMEM((2, CH, 5 * CH), bf16),
            pltpu.VMEM((2, CH, CH), bf16),
            pltpu.VMEM((CH, POS), f32),
            pltpu.VMEM((CH, POS), bf16),
            pltpu.VMEM((CH, POS), f32),
            pltpu.VMEM((2, 5 * CH, CH), bf16),
            pltpu.VMEM((2, CH, CH), bf16),
            pltpu.VMEM((4, CH, CH), f32),
            pltpu.VMEM((POS, CH), f32),
            pltpu.VMEM((DEV, 2 * TILES, CH), bf16),
            pltpu.VMEM((2, DEV, 2 * TILES, CH), bf16),
            pltpu.VMEM((N, N), bf16),
            pltpu.VMEM((N, N), bf16),
            pltpu.VMEM((N, N), bf16),
            pltpu.VMEM((DEV, TILES, CH), bf16),
            pltpu.VMEM((2, DEV, TILES, CH), bf16),
            pltpu.SemaphoreType.DMA((4,)),
            pltpu.SemaphoreType.DMA((4,)),
            pltpu.SemaphoreType.DMA((2, 5)),
        ],
        compiler_params=pltpu.CompilerParams(
            collective_id=0, has_side_effects=True, vmem_limit_bytes=40 << 20
        ),
    )(*[pltpu.with_memory_space_constraint(v, pltpu.HBM) for v in (pair.reshape(POS, CH), gain.reshape(4, CH), weight, weight_out)])
    return result.reshape(A, B, CH)


def solution(mesh):
    placed = (P("row", "col", None), P(), P(), P())
    return jax.shard_map(
        shards, mesh=mesh, in_specs=placed, out_specs=P("row", "col", None), check_vma=False
    )
```

```python
import jax
import jax.numpy as jnp
from jax import lax
from jax.experimental import pallas as pl
from jax.experimental.pallas import tpu as pltpu
from jax.sharding import PartitionSpec as P

LOGICAL = pl.DeviceIdType.LOGICAL
FAR_FIRST = (2, 3, 1, 0)
ROWS, COLS = 8, 16
DEV = ROWS * COLS
CHIPS = DEV // 2
A, B = 64, 32
CH = 128
POS = A * B
TILES = 16
N = 512
PER = 16
WIDE = 512
STEPS = POS // WIDE
APART = 40
CLOSE = 24
PLANE = DEV // 4
SUB = WIDE // CH


def sigmoid(x):
    return 0.5 * jnp.tanh(0.5 * x) + 0.5


def layer_norm(x, gain):
    center = jnp.mean(x, axis=0, keepdims=True)
    shifted = x - center
    spread = jnp.mean(shifted * shifted, axis=0, keepdims=True)
    return shifted * lax.rsqrt(spread + 1e-05) * gain


def swap_halves(v0, v1):
    h = CH // 2
    return (
        jnp.concatenate([v0[:, :h], v1[:, :h]], axis=1),
        jnp.concatenate([v0[:, h:], v1[:, h:]], axis=1),
    )


def dot(a, b):
    return jnp.dot(a, b, preferred_element_type=jnp.float32)


def kernel(pair_in, gain_in, weight_in, weight_out_in, out, pair, gain, weight, weight_out, state,
           normed, gate, wt, wot, gcol, wide, send, recv, xl, xr, turned, tri_send, tri_recv, in_sem,
           send_sem, recv_sem):
    r, c = lax.axis_index("row"), lax.axis_index("col")
    me = r * COLS + c
    chip, core = lax.div(me, 2), lax.rem(me, 2)

    loads = [
        pltpu.make_async_copy(x, y, in_sem.at[i])
        for i, (x, y) in enumerate(
            ((weight_in, weight), (gain_in, gain), (pair_in, pair), (weight_out_in, weight_out))
        )
    ]
    for load in loads:
        load.start()

    x, y, z = lax.div(c, 4), lax.rem(lax.div(c, 2), 2) * 2 + lax.div(r, 4), lax.rem(r, 4)
    mine = (core * 4 + x) * PER + r * 2 + lax.div(y, 2)

    def in_y(k):
        at = lax.rem(y + k, 4)
        lo, hi = lax.rem(at, 2), lax.div(at, 2)
        return lo * 32 + hi, lo * 8 + hi

    along_x = [lax.rem(x + k, 4) for k in FAR_FIRST]
    along_y = [in_y(k) for k in FAR_FIRST]

    def tour(i, visit):
        def stop(far, ks):
            at = lax.rem(z + far, 4)
            for k in ks:
                visit(along_x[i] * 2 + at * 8 + along_y[k][0], at * 2 + along_y[k][1])

        def plane(j, _):
            stop(2 + j - lax.div(j, 2) * (2 * j - 1), range(4))
            return 0

        lax.fori_loop(0, 4 if i < 3 else 3, plane, 0)
        if i == 3:
            stop(0, range(3))

    barrier = pltpu.get_barrier_semaphore()

    def greet(g):
        def visit(other, place):
            pl.semaphore_signal(barrier, inc=1, device_id=other * 2 + g, device_id_type=LOGICAL)

        for i in range(4):
            tour(i, visit)

    greet(0)
    greet(1)
    pl.semaphore_signal(barrier, inc=1, device_id=chip * 2 + 1 - core, device_id_type=LOGICAL)

    def ready():
        pl.semaphore_wait(barrier, DEV - 1)

    def spread(src, dst, sends, recvs, g, i):
        def visit(other, place):
            pltpu.make_async_remote_copy(
                src_ref=src(other, place), dst_ref=dst, send_sem=sends, recv_sem=recvs,
                device_id=other * 2 + g, device_id_type=LOGICAL,
            ).start()

        tour(i, visit)
        if i == 3:
            place = r * 2 + lax.div(y, 2)

            @pl.when(core == g)
            def _():
                pltpu.make_async_copy(src(chip, place), dst, recvs).start()

            @pl.when(core != g)
            def _():
                visit(chip, place)

    slot = r * 4 + lax.rem(c, 4)

    def spread_channels(g, i, u):
        spread(
            lambda other, place: send.at[(g * 4 + i) * PER + place], recv.at[u, i * PLANE + slot],
            send_sem.at[2 * u], recv_sem.at[u, i], g, i,
        )

    def spread_tri(g, i, u):
        spread(
            lambda other, place: tri_send.at[other * 2 + g], tri_recv.at[u, mine],
            send_sem.at[2 * u + 1], recv_sem.at[u, 4], g, i,
        )

    def arrived(dst, sem):
        pltpu.make_async_copy(dst, dst, sem).wait()

    def left(src, step):
        rest = src.at[pl.ds(0, DEV - 1)]
        pltpu.make_async_copy(rest, rest, send_sem.at[step]).wait()

    def turn(u):
        whole = jnp.transpose(weight[u])
        for n in range(CH // PER):
            for k in range(4):
                wt[u, (4 * n + k) * PER : (4 * n + k + 1) * PER] = whole[k * CH + n * PER : k * CH + (n + 1) * PER]
        wt[u, 4 * CH :] = whole[4 * CH :]
        wot[u] = jnp.transpose(weight_out[u])
        for k in range(2):
            gcol[2 * u + k] = jnp.transpose(jnp.broadcast_to(gain[2 * u + k : 2 * u + k + 1, :], (CH, CH)))

    loads[0].wait()
    loads[1].wait()
    loads[3].wait()
    turn(0)
    loads[2].wait()
    for s in range(TILES):
        rows = jnp.concatenate([pair[pl.ds(p * TILES + s, A, stride=B), :] for p in range(2)], axis=0)
        values = jnp.transpose(rows)
        state[:, s * CH : (s + 1) * CH] = values
        normed[:, s * CH : (s + 1) * CH] = layer_norm(values, gcol[0]).astype(jnp.bfloat16)

    for u in range(2):
        for n in range(4):
            g, first = n // 2, n % 2 * 2
            w = jnp.concatenate(
                [
                    wt[u, pl.ds(pl.multiple_of((g * 4 + along_x[i]) * 4 * PER, 4 * PER), 4 * PER), :]
                    for i in (first, first + 1)
                ],
                axis=0,
            )
            base = n % 2 * 2 * PER * APART
            for m in range(STEPS):
                proj = dot(w, normed[:, m * WIDE : (m + 1) * WIDE])
                for e in range(2):
                    part = [proj[(4 * e + k) * PER : (4 * e + k + 1) * PER] for k in range(4)]
                    both = (sigmoid(part[0]) * part[1], sigmoid(part[2]) * part[3])
                    for h in range(SUB):
                        for k in range(2):
                            wide[pl.ds(base + e * APART * PER + k * TILES + m * SUB + h, PER, stride=APART), :] = (
                                both[k][:, h * CH : (h + 1) * CH]
                            )
            if n == 0 and u == 1:
                left(send, 0)
            for i in (first, first + 1):
                for k in range(PER):
                    rows = wide[pl.ds(base + ((i - first) * PER + k) * APART, 2 * TILES), :]
                    send[(g * 4 + i) * PER + k] = rows.astype(jnp.bfloat16)
            if n == 1 and u == 0:
                ready()
            if n % 2 == 1:
                for i in range(4):
                    spread_channels(g, i, u)

        def open_gate(n, _):
            at = pl.ds(pl.multiple_of(n * WIDE, WIDE), WIDE)
            gate[:, at] = sigmoid(dot(wt[u, 4 * CH :], normed[:, at]))
            return 0

        lax.fori_loop(0, STEPS, open_gate, 0, unroll=True)
        if u == 0:
            turn(1)
        for i, k in enumerate(FAR_FIRST):
            arrived(recv.at[u, pl.ds(i * PLANE, PLANE)], recv_sem.at[u, i])
            top = lax.rem(x + 4 - k, 4) * CH

            def join(cc, _):
                at = pl.multiple_of(top + cc * B, B)
                for rp in range(4):
                    t0 = recv[u, i * PLANE + 2 * rp * 4 + cc]
                    t1 = recv[u, i * PLANE + (2 * rp + 1) * 4 + cc]
                    for m, lo in ((xl, 0), (xr, TILES)):
                        p0, p1 = swap_halves(t0[lo : lo + TILES], t1[lo : lo + TILES])
                        m[pl.ds(at, TILES), rp * CH : (rp + 1) * CH] = p0
                        m[pl.ds(pl.multiple_of(at + TILES, TILES), TILES), rp * CH : (rp + 1) * CH] = p1
                return 0

            lax.fori_loop(0, 4, join, 0, unroll=True)
            block = pl.ds(pl.multiple_of(top, CH), CH)
            turned[:, block] = jnp.transpose((xr if u == 0 else xl)[block, :])

        if u == 1:
            left(tri_send, 1)
        for h in range(4):
            rows = pl.ds(h * CH, CH)
            if u == 0:
                tri = dot(turned[rows, :], xl[...]).astype(jnp.bfloat16)
            else:
                tri = dot(xr[rows, :], turned[...]).astype(jnp.bfloat16)
            for i in range(4):
                cc = h * 4 + i
                for rp in range(4):
                    q0 = tri[i * B : i * B + TILES, rp * CH : (rp + 1) * CH]
                    q1 = tri[i * B + TILES : (i + 1) * B, rp * CH : (rp + 1) * CH]
                    p0, p1 = swap_halves(q0, q1)
                    tri_send[2 * rp * COLS + cc] = p0
                    tri_send[(2 * rp + 1) * COLS + cc] = p1
        for g in (0, 1) if u == 0 else (1, 0):
            for i in range(4):
                spread_tri(g, i, u)
        arrived(tri_recv.at[u], recv_sem.at[u, 4])

        def unpack(n, _):
            for k in range(16):
                at = pl.multiple_of((n * 16 + k) * CLOSE, 8)
                wide[pl.ds(at, TILES), :] = tri_recv[u, n * 16 + k].astype(jnp.float32)
            return 0

        lax.fori_loop(0, CH // 16, unpack, 0)

        def finish(n, _):
            at = pl.ds(pl.multiple_of(n * WIDE, WIDE), WIDE)
            outnorm = [
                layer_norm(wide[pl.ds(n * SUB + h, CH, stride=CLOSE), :], gcol[2 * u + 1]).astype(jnp.bfloat16)
                for h in range(SUB)
            ]
            new = state[:, at] + gate[:, at] * dot(wot[u], jnp.concatenate(outnorm, axis=1))
            if u == 0:
                state[:, at] = new
            for h in range(SUB):
                part = new[:, h * CH : (h + 1) * CH]
                if u == 0:
                    normed[:, pl.ds(pl.multiple_of(n * WIDE + h * CH, CH), CH)] = layer_norm(part, gcol[2]).astype(jnp.bfloat16)
                else:
                    rows = jnp.transpose(part)
                    for p in range(2):
                        out[pl.ds(p * TILES + n * SUB + h, A, stride=B), :] = rows[p * A : (p + 1) * A]
            return 0

        lax.fori_loop(0, STEPS, finish, 0, unroll=True)
    left(send, 2)
    left(tri_send, 3)


def shards(pair, gain, weight, weight_out):
    hbm = pl.BlockSpec(memory_space=pltpu.HBM)
    f32, bf16 = jnp.float32, jnp.bfloat16
    result = pl.pallas_call(
        kernel,
        out_shape=jax.ShapeDtypeStruct((POS, CH), f32),
        in_specs=[hbm] * 4,
        out_specs=pl.BlockSpec(memory_space=pltpu.VMEM),
        scratch_shapes=[
            pltpu.VMEM((POS, CH), f32),
            pltpu.VMEM((4, CH), f32),
            pltpu.VMEM((2, CH, 5 * CH), bf16),
            pltpu.VMEM((2, CH, CH), bf16),
            pltpu.VMEM((CH, POS), f32),
            pltpu.VMEM((CH, POS), bf16),
            pltpu.VMEM((CH, POS), f32),
            pltpu.VMEM((2, 5 * CH, CH), bf16),
            pltpu.VMEM((2, CH, CH), bf16),
            pltpu.VMEM((4, CH, CH), f32),
            pltpu.VMEM((CLOSE * CH, CH), f32),
            pltpu.VMEM((DEV, 2 * TILES, CH), bf16),
            pltpu.VMEM((2, DEV, 2 * TILES, CH), bf16),
            pltpu.VMEM((N, N), bf16),
            pltpu.VMEM((N, N), bf16),
            pltpu.VMEM((N, N), bf16),
            pltpu.VMEM((DEV, TILES, CH), bf16),
            pltpu.VMEM((2, DEV, TILES, CH), bf16),
            pltpu.SemaphoreType.DMA((4,)),
            pltpu.SemaphoreType.DMA((4,)),
            pltpu.SemaphoreType.DMA((2, 5)),
        ],
        compiler_params=pltpu.CompilerParams(
            collective_id=0, has_side_effects=True, vmem_limit_bytes=40 << 20
        ),
    )(*[pltpu.with_memory_space_constraint(v, pltpu.HBM) for v in (pair.reshape(POS, CH), gain.reshape(4, CH), weight, weight_out)])
    return result.reshape(A, B, CH)


def solution(mesh):
    placed = (P("row", "col", None), P(), P(), P())
    return jax.shard_map(
        shards, mesh=mesh, in_specs=placed, out_specs=P("row", "col", None), check_vma=False
    )
```

```python
import jax
import jax.numpy as jnp
from jax import lax
from jax.experimental import pallas as pl
from jax.experimental.pallas import tpu as pltpu
from jax.sharding import PartitionSpec as P

LOGICAL = pl.DeviceIdType.LOGICAL
FAR_FIRST = (2, 3, 1, 0)
ROWS, COLS = 8, 16
DEV = ROWS * COLS
CHIPS = DEV // 2
A, B = 64, 32
CH = 128
POS = A * B
TILES = 16
N = 512
PER = 16
WIDE = 512
STEPS = POS // WIDE
APART = 40
CLOSE = 24
PLANE = DEV // 4
SUB = WIDE // CH


def sigmoid(x):
    return 0.5 * jnp.tanh(0.5 * x) + 0.5


def layer_norm(x, gain):
    center = jnp.mean(x, axis=0, keepdims=True)
    shifted = x - center
    spread = jnp.mean(shifted * shifted, axis=0, keepdims=True)
    return shifted * lax.rsqrt(spread + 1e-05) * gain


def swap_halves(v0, v1):
    h = CH // 2
    return (
        jnp.concatenate([v0[:, :h], v1[:, :h]], axis=1),
        jnp.concatenate([v0[:, h:], v1[:, h:]], axis=1),
    )


def join_tiles(read, to, at):
    for k in range(4):
        lanes = pl.ds(k * CH, CH)
        p0, p1 = swap_halves(read(2 * k), read(2 * k + 1))
        to[pl.ds(at, TILES), lanes] = p0
        to[pl.ds(pl.multiple_of(at + TILES, TILES), TILES), lanes] = p1


def dot(a, b):
    return jnp.dot(a, b, preferred_element_type=jnp.float32)


def kernel(pair_in, gain_in, weight_in, weight_out_in, out, pair, gain, weight, weight_out, state,
           normed, gate, wt, wot, gcol, wide, send_a, send_b, send, recv_a, recv_b, recv, xl, xr, xf, turned, tri_send, tri_recv, in_sem,
           send_sem, recv_sem):
    r, c = lax.axis_index("row"), lax.axis_index("col")
    me = r * COLS + c
    chip, core = lax.div(me, 2), lax.rem(me, 2)

    loads = [
        pltpu.make_async_copy(x, y, in_sem.at[i])
        for i, (x, y) in enumerate(
            ((weight_in, weight), (gain_in, gain), (pair_in, pair), (weight_out_in, weight_out))
        )
    ]
    for load in loads:
        load.start()

    x, y, z = lax.div(c, 4), lax.rem(lax.div(c, 2), 2) * 2 + lax.div(r, 4), lax.rem(r, 4)
    mine = (core * 4 + x) * PER + r * 2 + lax.div(y, 2)

    def in_y(k):
        at = lax.rem(y + k, 4)
        lo, hi = lax.rem(at, 2), lax.div(at, 2)
        return lo * 32 + hi, lo * 8 + hi

    along_x = [lax.rem(x + k, 4) for k in FAR_FIRST]
    along_y = [in_y(k) for k in FAR_FIRST]

    def tour(i, visit):
        def stop(far, ks):
            at = lax.rem(z + far, 4)
            for k in ks:
                visit(along_x[i] * 2 + at * 8 + along_y[k][0], at * 2 + along_y[k][1])

        def plane(j, _):
            stop(2 + j - lax.div(j, 2) * (2 * j - 1), range(4))
            return 0

        lax.fori_loop(0, 4 if i < 3 else 3, plane, 0)
        if i == 3:
            stop(0, range(3))

    barrier = pltpu.get_barrier_semaphore()

    def greet(g):
        def visit(other, place):
            pl.semaphore_signal(barrier, inc=1, device_id=other * 2 + g, device_id_type=LOGICAL)

        for i in range(4):
            tour(i, visit)

    greet(0)
    greet(1)
    pl.semaphore_signal(barrier, inc=1, device_id=chip * 2 + 1 - core, device_id_type=LOGICAL)

    def ready():
        pl.semaphore_wait(barrier, DEV - 1)

    def spread(src, dst, sends, recvs, g, i):
        def visit(other, place):
            pltpu.make_async_remote_copy(
                src_ref=src(other, place), dst_ref=dst, send_sem=sends, recv_sem=recvs,
                device_id=other * 2 + g, device_id_type=LOGICAL,
            ).start()

        tour(i, visit)
        if i == 3:
            place = r * 2 + lax.div(y, 2)

            @pl.when(core == g)
            def _():
                pltpu.make_async_copy(src(chip, place), dst, recvs).start()

            @pl.when(core != g)
            def _():
                visit(chip, place)

    slot = r * 4 + lax.rem(c, 4)

    def spread_channels(g, i, u):
        src, dst = (send_a, recv_a) if u == 0 else (send, recv)
        spread(
            lambda other, place: src.at[(g * 4 + i) * PER + place], dst.at[i * PLANE + slot],
            send_sem.at[2 * u], recv_sem.at[u, i], g, i,
        )

    def spread_late(g, i):
        spread(
            lambda other, place: send_b.at[(g * 4 + i) * PER + place], recv_b.at[i * PLANE + slot],
            send_sem.at[4], recv_sem.at[2, i], g, i,
        )

    def spread_tri(g, i, u):
        spread(
            lambda other, place: tri_send.at[other * 2 + g], tri_recv.at[u, mine],
            send_sem.at[2 * u + 1], recv_sem.at[u, 4], g, i,
        )

    def arrived(dst, sem):
        pltpu.make_async_copy(dst, dst, sem).wait()

    def left(src, step):
        rest = src.at[pl.ds(0, DEV - 1)]
        pltpu.make_async_copy(rest, rest, send_sem.at[step]).wait()

    def turn(u):
        whole = jnp.transpose(weight[u])
        for n in range(CH // PER):
            for k in range(4):
                wt[u, (4 * n + k) * PER : (4 * n + k + 1) * PER] = whole[k * CH + n * PER : k * CH + (n + 1) * PER]
        wt[u, 4 * CH :] = whole[4 * CH :]
        wot[u] = jnp.transpose(weight_out[u])
        for k in range(2):
            gcol[2 * u + k] = jnp.transpose(jnp.broadcast_to(gain[2 * u + k : 2 * u + k + 1, :], (CH, CH)))

    loads[0].wait()
    loads[1].wait()
    loads[3].wait()
    turn(0)
    loads[2].wait()
    for s in range(TILES):
        rows = jnp.concatenate([pair[pl.ds(p * TILES + s, A, stride=B), :] for p in range(2)], axis=0)
        values = jnp.transpose(rows)
        state[:, s * CH : (s + 1) * CH] = values
        normed[:, s * CH : (s + 1) * CH] = layer_norm(values, gcol[0]).astype(jnp.bfloat16)

    for u in range(2):
        low = lax.rem(lax.broadcasted_iota(jnp.int32, (8, CH), 1), 2 * B) < B
        for n in range(4):
            g, first = n // 2, n % 2 * 2
            w = jnp.concatenate(
                [
                    wt[u, pl.ds(pl.multiple_of((g * 4 + along_x[i]) * 4 * PER, 4 * PER), 4 * PER), :]
                    for i in (first, first + 1)
                ],
                axis=0,
            )
            base = n % 2 * 2 * PER * APART
            for m in range(STEPS):
                proj = dot(w, normed[:, m * WIDE : (m + 1) * WIDE])
                for e in range(2):
                    part = [proj[(4 * e + k) * PER : (4 * e + k + 1) * PER] for k in range(4)]
                    both = (sigmoid(part[0]) * part[1], sigmoid(part[2]) * part[3])
                    for h in range(SUB):
                        for k in range(2):
                            wide[pl.ds(base + e * APART * PER + k * TILES + m * SUB + h, PER, stride=APART), :] = (
                                both[k][:, h * CH : (h + 1) * CH]
                            )
            for i in (first, first + 1):
                for k in range(PER):
                    start = base + ((i - first) * PER + k) * APART
                    at = (g * 4 + i) * PER + k
                    if u == 1:
                        send[at] = wide[pl.ds(start, 2 * TILES), :].astype(jnp.bfloat16)
                    else:
                        s0 = wide[pl.ds(start + TILES, 8), :]
                        s1 = wide[pl.ds(start + TILES + 8, 8), :]
                        first_half = jnp.where(low, s0, pltpu.roll(s1, B, 1))
                        second_half = jnp.where(low, pltpu.roll(s0, CH - B, 1), s1)
                        both = jnp.concatenate([wide[pl.ds(start, TILES), :], first_half], axis=0)
                        send_a[at] = both.astype(jnp.bfloat16)
                        send_b[at] = second_half.astype(jnp.bfloat16)
            if n == 1 and u == 0:
                ready()
            if n % 2 == 1:
                for i in range(4):
                    spread_channels(g, i, u)
        if u == 0:
            for n in range(8):
                spread_late(n // 4, n % 4)

        def open_gate(n, _):
            at = pl.ds(pl.multiple_of(n * WIDE, WIDE), WIDE)
            gate[:, at] = sigmoid(dot(wt[u, 4 * CH :], normed[:, at]))
            return 0

        lax.fori_loop(0, STEPS, open_gate, 0, unroll=True)
        if u == 0:
            turn(1)
        def join_half(src, i, cc, lo, top):
            for m in range(2):
                v = [src[i * PLANE + (4 * m + q) * 4 + cc, pl.ds(lo, 8), :].astype(jnp.float32) for q in range(4)]
                for k in range(4):
                    at = pl.multiple_of(top + cc * B + k * 8, 8)
                    xf[pl.ds(at, 8), m * CH : (m + 1) * CH] = jnp.concatenate(
                        [piece[:, k * B : (k + 1) * B] for piece in v], axis=1
                    )

        def send_half(half):
            for h in range(2):
                tri = dot(turned[pl.ds(h * CH, CH), :], xl[...]).astype(jnp.bfloat16)
                for q in range(4):
                    cc = 2 * (4 * h + q) + half
                    for rp in range(4):
                        q0 = tri[q * B : q * B + TILES, rp * CH : (rp + 1) * CH]
                        q1 = tri[q * B + TILES : (q + 1) * B, rp * CH : (rp + 1) * CH]
                        p0, p1 = swap_halves(q0, q1)
                        tri_send[2 * rp * COLS + cc] = p0
                        tri_send[(2 * rp + 1) * COLS + cc] = p1
            for i in range(4):
                spread_tri(half, i, u)

        for half in range(2 - u):
            for i, k in enumerate(FAR_FIRST):
                top = lax.rem(x + 4 - k, 4) * CH
                block = pl.ds(pl.multiple_of(top, CH), CH)
                plane = pl.ds(i * PLANE, PLANE)
                if u == 1:
                    arrived(recv.at[plane], recv_sem.at[1, i])
                elif half == 0:
                    arrived(recv_a.at[plane], recv_sem.at[0, i])
                else:
                    arrived(recv_b.at[plane], recv_sem.at[2, i])
                for cc in range(4):
                    at = pl.multiple_of(top + cc * B, B)
                    place = lambda row: i * PLANE + row * 4 + cc
                    if u == 1:
                        join_tiles(lambda row: recv[place(row), pl.ds(0, TILES), :], xl, at)
                        join_tiles(lambda row: recv[place(row), pl.ds(TILES, TILES), :], xr, at)
                    elif half == 0:
                        join_tiles(lambda row: recv_a[place(row), pl.ds(0, TILES), :], xl, at)
                        join_half(recv_a, i, cc, TILES, top)
                    else:
                        join_half(recv_b, i, cc, 0, top)
                if u == 1:
                    turned[:, block] = jnp.transpose(xl[block, :])
                else:
                    turned[0 : N // 2, block] = jnp.transpose(xf[block, :].astype(jnp.bfloat16))
            if u == 0:
                send_half(half)

        if u == 1:
            left(tri_send, 1)
            for h in range(4):
                tri = dot(xr[pl.ds(h * CH, CH), :], turned[...]).astype(jnp.bfloat16)
                for i in range(4):
                    cc = h * 4 + i
                    for rp in range(4):
                        q0 = tri[i * B : i * B + TILES, rp * CH : (rp + 1) * CH]
                        q1 = tri[i * B + TILES : (i + 1) * B, rp * CH : (rp + 1) * CH]
                        p0, p1 = swap_halves(q0, q1)
                        tri_send[2 * rp * COLS + cc] = p0
                        tri_send[(2 * rp + 1) * COLS + cc] = p1
            for g in (1, 0):
                for i in range(4):
                    spread_tri(g, i, u)
        arrived(tri_recv.at[u], recv_sem.at[u, 4])

        def unpack(n, _):
            for k in range(16):
                at = pl.multiple_of((n * 16 + k) * CLOSE, 8)
                wide[pl.ds(at, TILES), :] = tri_recv[u, n * 16 + k].astype(jnp.float32)
            return 0

        lax.fori_loop(0, CH // 16, unpack, 0)

        def finish(n, _):
            at = pl.ds(pl.multiple_of(n * WIDE, WIDE), WIDE)
            outnorm = [
                layer_norm(wide[pl.ds(n * SUB + h, CH, stride=CLOSE), :], gcol[2 * u + 1]).astype(jnp.bfloat16)
                for h in range(SUB)
            ]
            new = state[:, at] + gate[:, at] * dot(wot[u], jnp.concatenate(outnorm, axis=1))
            if u == 0:
                state[:, at] = new
            for h in range(SUB):
                part = new[:, h * CH : (h + 1) * CH]
                if u == 0:
                    normed[:, pl.ds(pl.multiple_of(n * WIDE + h * CH, CH), CH)] = layer_norm(part, gcol[2]).astype(jnp.bfloat16)
                else:
                    rows = jnp.transpose(part)
                    for p in range(2):
                        out[pl.ds(p * TILES + n * SUB + h, A, stride=B), :] = rows[p * A : (p + 1) * A]
            return 0

        lax.fori_loop(0, STEPS, finish, 0, unroll=True)
    left(send_a, 0)
    left(send_b, 4)
    left(send, 2)
    left(tri_send, 3)


def shards(pair, gain, weight, weight_out):
    hbm = pl.BlockSpec(memory_space=pltpu.HBM)
    f32, bf16 = jnp.float32, jnp.bfloat16
    result = pl.pallas_call(
        kernel,
        out_shape=jax.ShapeDtypeStruct((POS, CH), f32),
        in_specs=[hbm] * 4,
        out_specs=pl.BlockSpec(memory_space=pltpu.VMEM),
        scratch_shapes=[
            pltpu.VMEM((POS, CH), f32),
            pltpu.VMEM((4, CH), f32),
            pltpu.VMEM((2, CH, 5 * CH), bf16),
            pltpu.VMEM((2, CH, CH), bf16),
            pltpu.VMEM((CH, POS), f32),
            pltpu.VMEM((CH, POS), bf16),
            pltpu.VMEM((CH, POS), f32),
            pltpu.VMEM((2, 5 * CH, CH), bf16),
            pltpu.VMEM((2, CH, CH), bf16),
            pltpu.VMEM((4, CH, CH), f32),
            pltpu.VMEM((CLOSE * CH, CH), f32),
            pltpu.VMEM((DEV, TILES + 8, CH), bf16),
            pltpu.VMEM((DEV, 8, CH), bf16),
            pltpu.VMEM((DEV, 2 * TILES, CH), bf16),
            pltpu.VMEM((DEV, TILES + 8, CH), bf16),
            pltpu.VMEM((DEV, 8, CH), bf16),
            pltpu.VMEM((DEV, 2 * TILES, CH), bf16),
            pltpu.VMEM((N, N), bf16),
            pltpu.VMEM((N, N), bf16),
            pltpu.VMEM((N, N // 2), f32),
            pltpu.VMEM((N, N), bf16),
            pltpu.VMEM((DEV, TILES, CH), bf16),
            pltpu.VMEM((2, DEV, TILES, CH), bf16),
            pltpu.SemaphoreType.DMA((4,)),
            pltpu.SemaphoreType.DMA((5,)),
            pltpu.SemaphoreType.DMA((3, 5)),
        ],
        compiler_params=pltpu.CompilerParams(
            collective_id=0, has_side_effects=True, vmem_limit_bytes=40 << 20
        ),
    )(*[pltpu.with_memory_space_constraint(v, pltpu.HBM) for v in (pair.reshape(POS, CH), gain.reshape(4, CH), weight, weight_out)])
    return result.reshape(A, B, CH)


def solution(mesh):
    placed = (P("row", "col", None), P(), P(), P())
    return jax.shard_map(
        shards, mesh=mesh, in_specs=placed, out_specs=P("row", "col", None), check_vma=False
    )
```

```python
import jax
import jax.numpy as jnp
from jax import lax
from jax.experimental import pallas as pl
from jax.experimental.pallas import tpu as pltpu
from jax.sharding import PartitionSpec as P

LOGICAL = pl.DeviceIdType.LOGICAL
FAR_FIRST = (2, 3, 1, 0)
ROWS, COLS = 8, 16
DEV = ROWS * COLS
CHIPS = DEV // 2
A, B = 64, 32
CH = 128
POS = A * B
TILES = 16
N = 512
PER = 16
WIDE = 512
STEPS = POS // WIDE
APART = 40
CLOSE = 24
FAR = 136
PLANE = DEV // 4
SUB = WIDE // CH


def sigmoid(x):
    return 0.5 * jnp.tanh(0.5 * x) + 0.5


def layer_norm(x, gain):
    center = jnp.mean(x, axis=0, keepdims=True)
    shifted = x - center
    spread = jnp.mean(shifted * shifted, axis=0, keepdims=True)
    return shifted * lax.rsqrt(spread + 1e-05) * gain


def swap_halves(v0, v1):
    h = CH // 2
    return (
        jnp.concatenate([v0[:, :h], v1[:, :h]], axis=1),
        jnp.concatenate([v0[:, h:], v1[:, h:]], axis=1),
    )


def join_tiles(read, to, at):
    for k in range(4):
        lanes = pl.ds(k * CH, CH)
        p0, p1 = swap_halves(read(2 * k), read(2 * k + 1))
        to[pl.ds(at, TILES), lanes] = p0
        to[pl.ds(pl.multiple_of(at + TILES, TILES), TILES), lanes] = p1


def dot(a, b):
    return jnp.dot(a, b, preferred_element_type=jnp.float32)


def kernel(pair_in, gain_in, weight_in, weight_out_in, out, pair, gain, weight, weight_out, state,
           normed, gate, wt, wot, gcol, wide, wide_out, send_a, send_b, send, recv_a, recv_b, recv, xl, xr, xf, turned, tri_send, tri_recv, in_sem,
           send_sem, recv_sem):
    r, c = lax.axis_index("row"), lax.axis_index("col")
    me = r * COLS + c
    chip, core = lax.div(me, 2), lax.rem(me, 2)

    loads = [
        pltpu.make_async_copy(x, y, in_sem.at[i])
        for i, (x, y) in enumerate(
            ((weight_in, weight), (gain_in, gain), (pair_in, pair), (weight_out_in, weight_out))
        )
    ]
    for load in loads:
        load.start()

    x, y, z = lax.div(c, 4), lax.rem(lax.div(c, 2), 2) * 2 + lax.div(r, 4), lax.rem(r, 4)
    mine = (core * 4 + x) * PER + r * 2 + lax.div(y, 2)

    def in_y(k):
        at = lax.rem(y + k, 4)
        lo, hi = lax.rem(at, 2), lax.div(at, 2)
        return lo * 32 + hi, lo * 8 + hi

    along_x = [lax.rem(x + k, 4) for k in FAR_FIRST]
    along_y = [in_y(k) for k in FAR_FIRST]

    def tour(i, visit):
        def stop(far, ks):
            at = lax.rem(z + far, 4)
            for k in ks:
                visit(along_x[i] * 2 + at * 8 + along_y[k][0], at * 2 + along_y[k][1])

        def plane(j, _):
            stop(2 + j - lax.div(j, 2) * (2 * j - 1), range(4))
            return 0

        lax.fori_loop(0, 4 if i < 3 else 3, plane, 0)
        if i == 3:
            stop(0, range(3))

    barrier = pltpu.get_barrier_semaphore()

    def greet(g):
        def visit(other, place):
            pl.semaphore_signal(barrier, inc=1, device_id=other * 2 + g, device_id_type=LOGICAL)

        for i in range(4):
            tour(i, visit)

    greet(0)
    greet(1)
    pl.semaphore_signal(barrier, inc=1, device_id=chip * 2 + 1 - core, device_id_type=LOGICAL)

    def ready():
        pl.semaphore_wait(barrier, DEV - 1)

    def spread(src, dst, sends, recvs, g, i):
        def visit(other, place):
            pltpu.make_async_remote_copy(
                src_ref=src(other, place), dst_ref=dst, send_sem=sends, recv_sem=recvs,
                device_id=other * 2 + g, device_id_type=LOGICAL,
            ).start()

        tour(i, visit)
        if i == 3:
            place = r * 2 + lax.div(y, 2)

            @pl.when(core == g)
            def _():
                pltpu.make_async_copy(src(chip, place), dst, recvs).start()

            @pl.when(core != g)
            def _():
                visit(chip, place)

    slot = core * PER + r * 2 + lax.div(y, 2)

    def spread_channels(g, i, u):
        src, dst = (send_a, recv_a) if u == 0 else (send, recv)
        spread(
            lambda other, place: src.at[(g * 4 + i) * PER + place], dst.at[i * PLANE + slot],
            send_sem.at[2 * u], recv_sem.at[u, i], g, i,
        )

    def spread_part(g, i, rows, sem):
        spread(
            lambda other, place: send.at[(g * 4 + i) * PER + place, rows], recv.at[i * PLANE + slot, rows],
            send_sem.at[2], recv_sem.at[sem, i], g, i,
        )

    def spread_late(g, i):
        spread(
            lambda other, place: send_b.at[(g * 4 + i) * PER + place], recv_b.at[i * PLANE + slot],
            send_sem.at[4], recv_sem.at[2, i], g, i,
        )

    def spread_tri(g, i, u):
        spread(
            lambda other, place: tri_send.at[other * 2 + g], tri_recv.at[u, mine],
            send_sem.at[2 * u + 1], recv_sem.at[u, 4], g, i,
        )

    def arrived(dst, sem):
        pltpu.make_async_copy(dst, dst, sem).wait()

    def left(src, step):
        rest = src.at[pl.ds(0, DEV - 1)]
        pltpu.make_async_copy(rest, rest, send_sem.at[step]).wait()

    def turn(u):
        whole = jnp.transpose(weight[u])
        for n in range(CH // PER):
            for k in range(4):
                wt[u, (4 * n + k) * PER : (4 * n + k + 1) * PER] = whole[k * CH + n * PER : k * CH + (n + 1) * PER]
        wt[u, 4 * CH :] = whole[4 * CH :]
        wot[u] = jnp.transpose(weight_out[u])
        for k in range(2):
            gcol[2 * u + k] = jnp.transpose(jnp.broadcast_to(gain[2 * u + k : 2 * u + k + 1, :], (CH, CH)))

    loads[0].wait()
    loads[1].wait()
    loads[3].wait()
    turn(0)
    loads[2].wait()
    for s in range(TILES):
        rows = jnp.concatenate([pair[pl.ds(p * TILES + s, A, stride=B), :] for p in range(2)], axis=0)
        values = jnp.transpose(rows)
        state[:, s * CH : (s + 1) * CH] = values
        normed[:, s * CH : (s + 1) * CH] = layer_norm(values, gcol[0]).astype(jnp.bfloat16)

    for u in range(2):
        low = lax.rem(lax.broadcasted_iota(jnp.int32, (8, CH), 1), 2 * B) < B
        for n in range(4):
            g, first = n // 2, n % 2 * 2
            w = jnp.concatenate(
                [
                    wt[u, pl.ds(pl.multiple_of((g * 4 + along_x[i]) * 4 * PER, 4 * PER), 4 * PER), :]
                    for i in (first, first + 1)
                ],
                axis=0,
            )
            base = n % 2 * 2 * PER * APART
            for m in range(STEPS):
                proj = dot(w, normed[:, m * WIDE : (m + 1) * WIDE])
                for e in range(2):
                    part = [proj[(4 * e + k) * PER : (4 * e + k + 1) * PER] for k in range(4)]
                    both = (sigmoid(part[0]) * part[1], sigmoid(part[2]) * part[3])
                    for h in range(SUB):
                        for k in range(2):
                            wide[pl.ds(base + e * APART * PER + k * TILES + m * SUB + h, PER, stride=APART), :] = (
                                both[k][:, h * CH : (h + 1) * CH]
                            )
            for i in (first, first + 1):
                for k in range(PER):
                    start = base + ((i - first) * PER + k) * APART
                    at = (g * 4 + i) * PER + k
                    if u == 1:
                        send[at] = wide[pl.ds(start, 2 * TILES), :].astype(jnp.bfloat16)
                    else:
                        s0 = wide[pl.ds(start + TILES, 8), :]
                        s1 = wide[pl.ds(start + TILES + 8, 8), :]
                        first_half = jnp.where(low, s0, pltpu.roll(s1, B, 1))
                        second_half = jnp.where(low, pltpu.roll(s0, CH - B, 1), s1)
                        both = jnp.concatenate([wide[pl.ds(start, TILES), :], first_half], axis=0)
                        send_a[at] = both.astype(jnp.bfloat16)
                        send_b[at] = second_half.astype(jnp.bfloat16)
            if n == 1 and u == 0:
                ready()
            if n % 2 == 1 and u == 0:
                for i in range(4):
                    spread_channels(g, i, u)
            if n % 2 == 1 and u == 1:
                @pl.when(core == 0)
                def _():
                    for i in range(4):
                        spread_channels(g, i, u)

                @pl.when(core == 1)
                def _():
                    for i in range(4):
                        spread_part(g, i, pl.ds(0, TILES), 1)

        if u == 0:
            for n in range(8):
                spread_late(n // 4, n % 4)
        else:
            @pl.when(core == 1)
            def _():
                for n in range(8):
                    spread_part(n // 4, n % 4, pl.ds(TILES, TILES), 3)


        def open_gate(n, _):
            at = pl.ds(pl.multiple_of(n * WIDE, WIDE), WIDE)
            gate[:, at] = sigmoid(dot(wt[u, 4 * CH :], normed[:, at]))
            return 0

        lax.fori_loop(0, STEPS, open_gate, 0, unroll=True)
        if u == 0:
            turn(1)
        def join_half(src, i, cc, lo, top):
            for m in range(2):
                v = [src[i * PLANE + cc % 2 * PER + (4 * m + q) * 2 + cc // 2, pl.ds(lo, 8), :].astype(jnp.float32) for q in range(4)]
                for k in range(4):
                    at = pl.multiple_of(top + cc * B + k * 8, 8)
                    xf[pl.ds(at, 8), m * CH : (m + 1) * CH] = jnp.concatenate(
                        [piece[:, k * B : (k + 1) * B] for piece in v], axis=1
                    )

        def send_half(half):
            for h in range(2):
                if u == 0:
                    tri = dot(turned[pl.ds(h * CH, CH), :], xl[...]).astype(jnp.bfloat16)
                else:
                    tri = dot(xr[pl.ds(half * N // 2 + h * CH, CH), :], turned[...]).astype(jnp.bfloat16)
                for q in range(4):
                    cc = 2 * (4 * h + q) + half
                    for rp in range(4):
                        q0 = tri[q * B : q * B + TILES, rp * CH : (rp + 1) * CH]
                        q1 = tri[q * B + TILES : (q + 1) * B, rp * CH : (rp + 1) * CH]
                        p0, p1 = swap_halves(q0, q1)
                        tri_send[2 * rp * COLS + cc] = p0
                        tri_send[(2 * rp + 1) * COLS + cc] = p1
            for i in range(4):
                spread_tri(half, i, u)

        for half in range(2):
            for i, k in enumerate(FAR_FIRST):
                far = lax.rem(x + 4 - k, 4)
                top = far * CH
                block = pl.ds(pl.multiple_of(top, CH), CH)
                plane = pl.ds(i * PLANE, PLANE)
                if u == 1 and half == 0:
                    arrived(recv.at[pl.ds(i * PLANE, PLANE * 3 // 4)], recv_sem.at[1, i])
                elif u == 1:
                    arrived(recv.at[pl.ds(i * PLANE, PLANE // 4)], recv_sem.at[3, i])
                elif half == 0:
                    arrived(recv_a.at[plane], recv_sem.at[0, i])
                else:
                    arrived(recv_b.at[plane], recv_sem.at[2, i])
                for cc in range(4):
                    at = pl.multiple_of(top + cc * B, B)
                    place = lambda row: i * PLANE + cc % 2 * PER + row * 2 + cc // 2
                    if u == 1:
                        if half == 0:
                            join_tiles(lambda row: recv[place(row), pl.ds(0, TILES), :], xl, at)
                        if cc % 2 == half:
                            to = pl.multiple_of(half * N // 2 + far * 2 * B + cc // 2 * B, B)
                            join_tiles(lambda row: recv[place(row), pl.ds(TILES, TILES), :], xr, to)
                    elif half == 0:
                        join_tiles(lambda row: recv_a[place(row), pl.ds(0, TILES), :], xl, at)
                        join_half(recv_a, i, cc, TILES, top)
                    else:
                        join_half(recv_b, i, cc, 0, top)
                if u == 1 and half == 0:
                    turned[:, block] = jnp.transpose(xl[block, :])
                elif u == 0:
                    turned[0 : N // 2, block] = jnp.transpose(xf[block, :].astype(jnp.bfloat16))
            if u == 1 and half == 0:
                left(tri_send, 1)
            send_half(half)

        arrived(tri_recv.at[u], recv_sem.at[u, 4])

        def unpack(n, _):
            for k in range(16):
                at = pl.multiple_of((n * 16 + k) * CLOSE, 8)
                wide[pl.ds(at, TILES), :] = tri_recv[u, n * 16 + k].astype(jnp.float32)
            return 0

        lax.fori_loop(0, CH // 16, unpack, 0)

        def finish(n, _):
            at = pl.ds(pl.multiple_of(n * WIDE, WIDE), WIDE)
            outnorm = [
                layer_norm(wide[pl.ds(n * SUB + h, CH, stride=CLOSE), :], gcol[2 * u + 1]).astype(jnp.bfloat16)
                for h in range(SUB)
            ]
            new = state[:, at] + gate[:, at] * dot(wot[u], jnp.concatenate(outnorm, axis=1))
            if u == 0:
                state[:, at] = new
            for h in range(SUB):
                part = new[:, h * CH : (h + 1) * CH]
                if u == 0:
                    normed[:, pl.ds(pl.multiple_of(n * WIDE + h * CH, CH), CH)] = layer_norm(part, gcol[2]).astype(jnp.bfloat16)
                else:
                    wide_out[pl.ds(pl.multiple_of((n * SUB + h) * FAR, 8), CH), :] = jnp.transpose(part)
            return 0

        lax.fori_loop(0, STEPS, finish, 0, unroll=True)

    def order(a, _):
        for k in range(4):
            p, o = k // 2, k % 2
            to = pl.multiple_of(a * B + k * 8, 8)
            out[pl.ds(to, 8), :] = wide_out[pl.ds(o * 8 * FAR + p * A + a, 8, stride=FAR), :]
        return 0

    lax.fori_loop(0, A, order, 0, unroll=16)
    left(send_a, 0)
    left(send_b, 4)
    left(send, 2)
    left(tri_send, 3)


def shards(pair, gain, weight, weight_out):
    hbm = pl.BlockSpec(memory_space=pltpu.HBM)
    f32, bf16 = jnp.float32, jnp.bfloat16
    result = pl.pallas_call(
        kernel,
        out_shape=jax.ShapeDtypeStruct((POS, CH), f32),
        in_specs=[hbm] * 4,
        out_specs=pl.BlockSpec(memory_space=pltpu.VMEM),
        scratch_shapes=[
            pltpu.VMEM((POS, CH), f32),
            pltpu.VMEM((4, CH), f32),
            pltpu.VMEM((2, CH, 5 * CH), bf16),
            pltpu.VMEM((2, CH, CH), bf16),
            pltpu.VMEM((CH, POS), f32),
            pltpu.VMEM((CH, POS), bf16),
            pltpu.VMEM((CH, POS), f32),
            pltpu.VMEM((2, 5 * CH, CH), bf16),
            pltpu.VMEM((2, CH, CH), bf16),
            pltpu.VMEM((4, CH, CH), f32),
            pltpu.VMEM((CLOSE * CH, CH), f32),
            pltpu.VMEM((FAR * TILES, CH), f32),
            pltpu.VMEM((DEV, TILES + 8, CH), bf16),
            pltpu.VMEM((DEV, 8, CH), bf16),
            pltpu.VMEM((DEV, 2 * TILES, CH), bf16),
            pltpu.VMEM((DEV, TILES + 8, CH), bf16),
            pltpu.VMEM((DEV, 8, CH), bf16),
            pltpu.VMEM((DEV, 2 * TILES, CH), bf16),
            pltpu.VMEM((N, N), bf16),
            pltpu.VMEM((N, N), bf16),
            pltpu.VMEM((N, N // 2), f32),
            pltpu.VMEM((N, N), bf16),
            pltpu.VMEM((DEV, TILES, CH), bf16),
            pltpu.VMEM((2, DEV, TILES, CH), bf16),
            pltpu.SemaphoreType.DMA((4,)),
            pltpu.SemaphoreType.DMA((5,)),
            pltpu.SemaphoreType.DMA((4, 5)),
        ],
        compiler_params=pltpu.CompilerParams(
            collective_id=0, has_side_effects=True, vmem_limit_bytes=40 << 20
        ),
    )(*[pltpu.with_memory_space_constraint(v, pltpu.HBM) for v in (pair.reshape(POS, CH), gain.reshape(4, CH), weight, weight_out)])
    return result.reshape(A, B, CH)


def solution(mesh):
    placed = (P("row", "col", None), P(), P(), P())
    return jax.shard_map(
        shards, mesh=mesh, in_specs=placed, out_specs=P("row", "col", None), check_vma=False
    )
```

```python
import jax
import jax.numpy as jnp
from jax import lax
from jax.experimental import pallas as pl
from jax.experimental.pallas import tpu as pltpu
from jax.sharding import PartitionSpec as P

LOGICAL = pl.DeviceIdType.LOGICAL
FAR_FIRST = (2, 3, 1, 0)
ROWS, COLS = 8, 16
DEV = ROWS * COLS
CHIPS = DEV // 2
A, B = 64, 32
CH = 128
POS = A * B
TILES = 16
N = 512
PER = 16
WIDE = 512
STEPS = POS // WIDE
APART = 40
CLOSE = 24
FAR = 136
PLANE = DEV // 4
SUB = WIDE // CH


def sigmoid(x):
    return 0.5 * jnp.tanh(0.5 * x) + 0.5


def layer_norm(x, gain):
    center = jnp.mean(x, axis=0, keepdims=True)
    shifted = x - center
    spread = jnp.mean(shifted * shifted, axis=0, keepdims=True)
    return shifted * lax.rsqrt(spread + 1e-05) * gain


def swap_halves(v0, v1):
    h = CH // 2
    return (
        jnp.concatenate([v0[:, :h], v1[:, :h]], axis=1),
        jnp.concatenate([v0[:, h:], v1[:, h:]], axis=1),
    )


def join_tiles(read, to, at):
    for k in range(4):
        lanes = pl.ds(k * CH, CH)
        p0, p1 = swap_halves(read(2 * k), read(2 * k + 1))
        to[pl.ds(at, TILES), lanes] = p0
        to[pl.ds(pl.multiple_of(at + TILES, TILES), TILES), lanes] = p1


def dot(a, b):
    return jnp.dot(a, b, preferred_element_type=jnp.float32)


def kernel(pair_in, gain_in, weight_in, weight_out_in, out, pair, gain, weight, weight_out, state,
           normed, gate, wt, wot, gcol, wide, wide_out, send_a, send_b, send, recv_a, recv_b, recv, xl, xr, xf, turned, tri_send, tri_recv, in_sem,
           send_sem, recv_sem):
    r, c = lax.axis_index("row"), lax.axis_index("col")
    me = r * COLS + c
    chip, core = lax.div(me, 2), lax.rem(me, 2)

    loads = [
        pltpu.make_async_copy(x, y, in_sem.at[i])
        for i, (x, y) in enumerate(
            ((weight_in, weight), (gain_in, gain), (pair_in, pair), (weight_out_in, weight_out))
        )
    ]
    loads[2].start()

    x, y, z = lax.div(c, 4), lax.rem(lax.div(c, 2), 2) * 2 + lax.div(r, 4), lax.rem(r, 4)
    mine = (core * 4 + x) * PER + r * 2 + lax.div(y, 2)

    def in_y(k):
        at = lax.rem(y + k, 4)
        lo, hi = lax.rem(at, 2), lax.div(at, 2)
        return lo * 32 + hi, lo * 8 + hi

    along_x = [lax.rem(x + k, 4) for k in FAR_FIRST]
    along_y = [in_y(k) for k in FAR_FIRST]

    def tour(i, visit):
        def stop(far, ks):
            at = lax.rem(z + far, 4)
            for k in ks:
                visit(along_x[i] * 2 + at * 8 + along_y[k][0], at * 2 + along_y[k][1])

        def plane(j, _):
            stop(2 + j - lax.div(j, 2) * (2 * j - 1), range(4))
            return 0

        lax.fori_loop(0, 4 if i < 3 else 3, plane, 0)
        if i == 3:
            stop(0, range(3))

    barrier = pltpu.get_barrier_semaphore()

    def greet(g):
        def visit(other, place):
            pl.semaphore_signal(barrier, inc=1, device_id=other * 2 + g, device_id_type=LOGICAL)

        for i in range(4):
            tour(i, visit)

    greet(0)
    greet(1)
    for i in (0, 1, 3):
        loads[i].start()
    pl.semaphore_signal(barrier, inc=1, device_id=chip * 2 + 1 - core, device_id_type=LOGICAL)

    def ready():
        pl.semaphore_wait(barrier, DEV - 1)

    def spread(src, dst, sends, recvs, g, i):
        def visit(other, place):
            pltpu.make_async_remote_copy(
                src_ref=src(other, place), dst_ref=dst, send_sem=sends, recv_sem=recvs,
                device_id=other * 2 + g, device_id_type=LOGICAL,
            ).start()

        tour(i, visit)
        if i == 3:
            place = r * 2 + lax.div(y, 2)

            @pl.when(core == g)
            def _():
                pltpu.make_async_copy(src(chip, place), dst, recvs).start()

            @pl.when(core != g)
            def _():
                visit(chip, place)

    slot = core * PER + r * 2 + lax.div(y, 2)

    def spread_channels(g, i, u):
        src, dst = (send_a, recv_a) if u == 0 else (send, recv)
        spread(
            lambda other, place: src.at[(g * 4 + i) * PER + place], dst.at[i * PLANE + slot],
            send_sem.at[2 * u], recv_sem.at[u, i], g, i,
        )

    def spread_part(g, i, rows, sem):
        spread(
            lambda other, place: send.at[(g * 4 + i) * PER + place, rows], recv.at[i * PLANE + slot, rows],
            send_sem.at[2], recv_sem.at[sem, i], g, i,
        )

    def spread_late(g, i):
        spread(
            lambda other, place: send_b.at[(g * 4 + i) * PER + place], recv_b.at[i * PLANE + slot],
            send_sem.at[4], recv_sem.at[2, i], g, i,
        )

    def spread_tri(g, i, u):
        spread(
            lambda other, place: tri_send.at[other * 2 + g], tri_recv.at[u, mine],
            send_sem.at[2 * u + 1], recv_sem.at[u, 4], g, i,
        )

    def arrived(dst, sem):
        pltpu.make_async_copy(dst, dst, sem).wait()

    def left(src, step):
        rest = src.at[pl.ds(0, DEV - 1)]
        pltpu.make_async_copy(rest, rest, send_sem.at[step]).wait()

    def turn(u):
        whole = jnp.transpose(weight[u])
        for n in range(CH // PER):
            for k in range(4):
                wt[u, (4 * n + k) * PER : (4 * n + k + 1) * PER] = whole[k * CH + n * PER : k * CH + (n + 1) * PER]
        wt[u, 4 * CH :] = whole[4 * CH :]
        wot[u] = jnp.transpose(weight_out[u])
        for k in range(2):
            gcol[2 * u + k] = jnp.transpose(jnp.broadcast_to(gain[2 * u + k : 2 * u + k + 1, :], (CH, CH)))

    loads[0].wait()
    loads[1].wait()
    loads[3].wait()
    turn(0)
    loads[2].wait()
    for s in range(TILES):
        rows = jnp.concatenate([pair[pl.ds(p * TILES + s, A, stride=B), :] for p in range(2)], axis=0)
        values = jnp.transpose(rows)
        state[:, s * CH : (s + 1) * CH] = values
        normed[:, s * CH : (s + 1) * CH] = layer_norm(values, gcol[0]).astype(jnp.bfloat16)

    for u in range(2):
        low = lax.rem(lax.broadcasted_iota(jnp.int32, (8, CH), 1), 2 * B) < B
        for n in range(4):
            g, first = n // 2, n % 2 * 2
            w = jnp.concatenate(
                [
                    wt[u, pl.ds(pl.multiple_of((g * 4 + along_x[i]) * 4 * PER, 4 * PER), 4 * PER), :]
                    for i in (first, first + 1)
                ],
                axis=0,
            )
            base = n % 2 * 2 * PER * APART
            for m in range(STEPS):
                proj = dot(w, normed[:, m * WIDE : (m + 1) * WIDE])
                for e in range(2):
                    part = [proj[(4 * e + k) * PER : (4 * e + k + 1) * PER] for k in range(4)]
                    both = (sigmoid(part[0]) * part[1], sigmoid(part[2]) * part[3])
                    for h in range(SUB):
                        for k in range(2):
                            wide[pl.ds(base + e * APART * PER + k * TILES + m * SUB + h, PER, stride=APART), :] = (
                                both[k][:, h * CH : (h + 1) * CH]
                            )
            for i in (first, first + 1):
                for k in range(PER):
                    start = base + ((i - first) * PER + k) * APART
                    at = (g * 4 + i) * PER + k
                    if u == 1:
                        send[at] = wide[pl.ds(start, 2 * TILES), :].astype(jnp.bfloat16)
                    else:
                        s0 = wide[pl.ds(start + TILES, 8), :]
                        s1 = wide[pl.ds(start + TILES + 8, 8), :]
                        first_half = jnp.where(low, s0, pltpu.roll(s1, B, 1))
                        second_half = jnp.where(low, pltpu.roll(s0, CH - B, 1), s1)
                        both = jnp.concatenate([wide[pl.ds(start, TILES), :], first_half], axis=0)
                        send_a[at] = both.astype(jnp.bfloat16)
                        send_b[at] = second_half.astype(jnp.bfloat16)
            if n == 1 and u == 0:
                ready()
            if n % 2 == 1 and u == 0:
                for i in range(4):
                    spread_channels(g, i, u)
            if n % 2 == 1 and u == 1:
                @pl.when(core == 0)
                def _():
                    for i in range(4):
                        spread_channels(g, i, u)

                @pl.when(core == 1)
                def _():
                    for i in range(4):
                        spread_part(g, i, pl.ds(0, TILES), 1)

        if u == 0:
            for n in range(8):
                spread_late(n // 4, n % 4)
        else:
            @pl.when(core == 1)
            def _():
                for n in range(8):
                    spread_part(n // 4, n % 4, pl.ds(TILES, TILES), 3)


        def open_gate(n, _):
            at = pl.ds(pl.multiple_of(n * WIDE, WIDE), WIDE)
            gate[:, at] = sigmoid(dot(wt[u, 4 * CH :], normed[:, at]))
            return 0

        lax.fori_loop(0, STEPS, open_gate, 0, unroll=True)
        if u == 0:
            turn(1)
        def join_half(src, i, cc, lo, top):
            for m in range(2):
                v = [src[i * PLANE + cc % 2 * PER + (4 * m + q) * 2 + cc // 2, pl.ds(lo, 8), :].astype(jnp.float32) for q in range(4)]
                for k in range(4):
                    at = pl.multiple_of(top + cc * B + k * 8, 8)
                    xf[pl.ds(at, 8), m * CH : (m + 1) * CH] = jnp.concatenate(
                        [piece[:, k * B : (k + 1) * B] for piece in v], axis=1
                    )

        def send_half(half):
            for h in range(2):
                if u == 0:
                    tri = dot(turned[pl.ds(h * CH, CH), :], xl[...]).astype(jnp.bfloat16)
                else:
                    tri = dot(xr[pl.ds(half * N // 2 + h * CH, CH), :], turned[...]).astype(jnp.bfloat16)
                for q in range(4):
                    cc = 2 * (4 * h + q) + half
                    for rp in range(4):
                        q0 = tri[q * B : q * B + TILES, rp * CH : (rp + 1) * CH]
                        q1 = tri[q * B + TILES : (q + 1) * B, rp * CH : (rp + 1) * CH]
                        p0, p1 = swap_halves(q0, q1)
                        tri_send[2 * rp * COLS + cc] = p0
                        tri_send[(2 * rp + 1) * COLS + cc] = p1
            for i in range(4):
                spread_tri(half, i, u)

        for half in range(2):
            for i, k in enumerate(FAR_FIRST):
                far = lax.rem(x + 4 - k, 4)
                top = far * CH
                block = pl.ds(pl.multiple_of(top, CH), CH)
                plane = pl.ds(i * PLANE, PLANE)
                if u == 1 and half == 0:
                    arrived(recv.at[pl.ds(i * PLANE, PLANE * 3 // 4)], recv_sem.at[1, i])
                elif u == 1:
                    arrived(recv.at[pl.ds(i * PLANE, PLANE // 4)], recv_sem.at[3, i])
                elif half == 0:
                    arrived(recv_a.at[plane], recv_sem.at[0, i])
                else:
                    arrived(recv_b.at[plane], recv_sem.at[2, i])
                for cc in range(4):
                    at = pl.multiple_of(top + cc * B, B)
                    place = lambda row: i * PLANE + cc % 2 * PER + row * 2 + cc // 2
                    if u == 1:
                        if half == 0:
                            join_tiles(lambda row: recv[place(row), pl.ds(0, TILES), :], xl, at)
                        if cc % 2 == half:
                            to = pl.multiple_of(half * N // 2 + far * 2 * B + cc // 2 * B, B)
                            join_tiles(lambda row: recv[place(row), pl.ds(TILES, TILES), :], xr, to)
                    elif half == 0:
                        join_tiles(lambda row: recv_a[place(row), pl.ds(0, TILES), :], xl, at)
                        join_half(recv_a, i, cc, TILES, top)
                    else:
                        join_half(recv_b, i, cc, 0, top)
                if u == 1 and half == 0:
                    turned[:, block] = jnp.transpose(xl[block, :])
                elif u == 0:
                    turned[0 : N // 2, block] = jnp.transpose(xf[block, :].astype(jnp.bfloat16))
            if u == 1 and half == 0:
                left(tri_send, 1)
            send_half(half)

        arrived(tri_recv.at[u], recv_sem.at[u, 4])

        def unpack(n, _):
            for k in range(16):
                at = pl.multiple_of((n * 16 + k) * CLOSE, 8)
                wide[pl.ds(at, TILES), :] = tri_recv[u, n * 16 + k].astype(jnp.float32)
            return 0

        lax.fori_loop(0, CH // 16, unpack, 0)

        def finish(n, _):
            at = pl.ds(pl.multiple_of(n * WIDE, WIDE), WIDE)
            outnorm = [
                layer_norm(wide[pl.ds(n * SUB + h, CH, stride=CLOSE), :], gcol[2 * u + 1]).astype(jnp.bfloat16)
                for h in range(SUB)
            ]
            new = state[:, at] + gate[:, at] * dot(wot[u], jnp.concatenate(outnorm, axis=1))
            if u == 0:
                state[:, at] = new
            for h in range(SUB):
                part = new[:, h * CH : (h + 1) * CH]
                if u == 0:
                    normed[:, pl.ds(pl.multiple_of(n * WIDE + h * CH, CH), CH)] = layer_norm(part, gcol[2]).astype(jnp.bfloat16)
                else:
                    wide_out[pl.ds(pl.multiple_of((n * SUB + h) * FAR, 8), CH), :] = jnp.transpose(part)
            return 0

        lax.fori_loop(0, STEPS, finish, 0, unroll=True)

    def order(a, _):
        for k in range(4):
            p, o = k // 2, k % 2
            to = pl.multiple_of(a * B + k * 8, 8)
            out[pl.ds(to, 8), :] = wide_out[pl.ds(o * 8 * FAR + p * A + a, 8, stride=FAR), :]
        return 0

    lax.fori_loop(0, A, order, 0, unroll=16)
    left(send_a, 0)
    left(send_b, 4)
    left(send, 2)
    left(tri_send, 3)


def shards(pair, gain, weight, weight_out):
    hbm = pl.BlockSpec(memory_space=pltpu.HBM)
    f32, bf16 = jnp.float32, jnp.bfloat16
    result = pl.pallas_call(
        kernel,
        out_shape=jax.ShapeDtypeStruct((POS, CH), f32),
        in_specs=[hbm] * 4,
        out_specs=pl.BlockSpec(memory_space=pltpu.VMEM),
        scratch_shapes=[
            pltpu.VMEM((POS, CH), f32),
            pltpu.VMEM((4, CH), f32),
            pltpu.VMEM((2, CH, 5 * CH), bf16),
            pltpu.VMEM((2, CH, CH), bf16),
            pltpu.VMEM((CH, POS), f32),
            pltpu.VMEM((CH, POS), bf16),
            pltpu.VMEM((CH, POS), f32),
            pltpu.VMEM((2, 5 * CH, CH), bf16),
            pltpu.VMEM((2, CH, CH), bf16),
            pltpu.VMEM((4, CH, CH), f32),
            pltpu.VMEM((CLOSE * CH, CH), f32),
            pltpu.VMEM((FAR * TILES, CH), f32),
            pltpu.VMEM((DEV, TILES + 8, CH), bf16),
            pltpu.VMEM((DEV, 8, CH), bf16),
            pltpu.VMEM((DEV, 2 * TILES, CH), bf16),
            pltpu.VMEM((DEV, TILES + 8, CH), bf16),
            pltpu.VMEM((DEV, 8, CH), bf16),
            pltpu.VMEM((DEV, 2 * TILES, CH), bf16),
            pltpu.VMEM((N, N), bf16),
            pltpu.VMEM((N, N), bf16),
            pltpu.VMEM((N, N // 2), f32),
            pltpu.VMEM((N, N), bf16),
            pltpu.VMEM((DEV, TILES, CH), bf16),
            pltpu.VMEM((2, DEV, TILES, CH), bf16),
            pltpu.SemaphoreType.DMA((4,)),
            pltpu.SemaphoreType.DMA((5,)),
            pltpu.SemaphoreType.DMA((4, 5)),
        ],
        compiler_params=pltpu.CompilerParams(
            collective_id=0, has_side_effects=True, vmem_limit_bytes=40 << 20
        ),
    )(*[pltpu.with_memory_space_constraint(v, pltpu.HBM) for v in (pair.reshape(POS, CH), gain.reshape(4, CH), weight, weight_out)])
    return result.reshape(A, B, CH)


def solution(mesh):
    placed = (P("row", "col", None), P(), P(), P())
    return jax.shard_map(
        shards, mesh=mesh, in_specs=placed, out_specs=P("row", "col", None), check_vma=False
    )
```
